128 devices in a mesh: bx: 8 (over y, core), by: 16 (over x, z).
Axes of the slice: x: 4, y: 4, z: 4, core: 2. Of those that a mesh axis runs over, the one named last changes fastest.
Arguments:
- initial_thermal_state: float32 [64, 524288], P(None, ('bx', 'by')), may hold values from -6 to 6
- baseline_diffusivity: float32 [64, 524288], P(None, ('bx', 'by')), may hold values from 0.3 to 3
- thermal_storage: float32 [64, 524288], P(None, ('bx', 'by')), may hold values from 0.5 to 4
- refinement_depth: int32 [524288], P(('bx', 'by')), may hold values from 0 to 2
- interface_voxel_table: int32 [128, 128, 32], P(('bx', 'by')), may hold values from 0 to 262143
- interface_weighting: float32 [128, 128, 32], P(('bx', 'by')), may hold values from 0.25 to 4, as said below
- laser_energy_deposits: float32 [1, 32768, 256], P(None, ('bx', 'by')), may hold values from 0 to 1
- laser_spot_holder: int32 [1, 32768, 1], P(None, ('bx', 'by')), may hold values from 0 to 127; in each aligned block of 256 rows (0 to 255, 256 to 511, ..., all dimensions but the last counted through in order) at most 8 rows name the same one
- laser_spot_patch: int32 [1, 32768], P(None, ('bx', 'by')), may hold values from 0 to 1023
Outputs:
- temperature_out: float32 [64, 524288], P(None, ('bx', 'by'))
- equation_misfit: float32 [64, 524288], P(None, ('bx', 'by'))
The draws below stay inside these ranges and needn't reach their ends.
Inputs may be any that keep to these rules, and one draw needn't show every extreme that they name: interface_weighting[p, q, s] equals interface_weighting[q, p, s]. `laser_spot_holder`: among the scan points of one step in the rows of one device, at most 8 name the same owner, and in every draw some owner is named exactly 8 times.
All inputs are finite; a program needn't handle non-finite values.
Results may differ from the reference program's by a relative error of at most 0.00026.
Values sent between devices are 32-bit elements; how exact they have to be, the bound alone decides.
A program may use at most 128 MiB of HBM per device.

```python
import math
import jax
import jax.numpy as jnp
import numpy as np

BLK_DEV = 4096
SLOTS = 32
PTS_DEV = 256
CAP = 8
ROW_W = 256
STEPS = 1
ITERS = 4
OWNERS = 128
OCTANT_NUMBER = 524288
TILES_DEV = 1024
POINTS = 32768


def draw_interface_weighting(key, part):
    key = jax.random.fold_in(key, 11)
    shape_all = (OWNERS, OWNERS, SLOTS)
    base_draw = jnp.exp(jax.random.uniform(key, shape_all, jnp.float32, -1.3862944, 1.3862944))
    return 0.5 * (base_draw + jnp.transpose(base_draw, (1, 0, 2)))


def place_ends(result, rng, low, top_value):
    index_at = [jax.random.randint(jax.random.fold_in(rng, axis), (), 0, length) for axis, length in enumerate(result.shape)]
    longest = result.shape.index(max(result.shape))
    neighbour = index_at[:longest] + [(index_at[longest] + 1) % result.shape[longest]] + index_at[longest + 1:]
    return result.at[tuple(index_at)].set(low).at[tuple(neighbour)].set(top_value)


def levels(stream_key, dims, cuts, least, high):
    def one(axis_at, parts):
        steps = jax.random.uniform(jax.random.fold_in(jax.random.fold_in(stream_key, 6), axis_at), (parts,), jnp.float32, least / len(cuts), high / len(cuts))
        return jnp.repeat(jnp.exp(steps), dims[axis_at] // parts).reshape((-1,) + (1,) * (len(dims) - axis_at - 1))

    loudness = one(*cuts[0])
    for cut in cuts[1:]:
        loudness = loudness * one(*cut)
    return loudness


def routed_block(key, own, number, rows, count, top, most, slope):
    sequence = jax.random.permutation(key, count)
    heavy_load, usual = shares(count, rows * top, most, slope, True), shares(count, rows * top, most, slope, False)
    places = jnp.arange(count)

    def named(sizes, offset_by):
        used = int((sizes > 0).sum())
        fixed = max(1, used // 4)
        moved = fixed + (places - fixed + offset_by * (used - fixed)) % max(1, count - fixed)
        return jnp.zeros((count,), jnp.int32).at[sequence[jnp.where(places < fixed, places, moved)]].set(jnp.asarray(sizes, jnp.int32))

    sizes = jnp.where(number % 4 == 0, named(heavy_load, number // 4), named(usual, number - number // 4 - 1))
    mixed = jax.random.permutation(jax.random.fold_in(own, 3), count)
    source_of, sink = mixed[0:count // 2 * 2:2], mixed[1:count // 2 * 2:2]
    margin = jnp.minimum(sizes[source_of] - 1, most - sizes[sink]) // 2
    margin = jnp.where((source_of == sequence[0]) | (sink == sequence[0]) | (sizes[sink] == 0), 0, jnp.maximum(margin, 0))
    moved = jax.random.randint(jax.random.fold_in(own, 4), (count // 2,), 0, 1 << 20) % (margin + 1)
    sizes = sizes.at[source_of].add(-moved).at[sink].add(moved)
    items = jnp.searchsorted(jnp.cumsum(sizes), jnp.arange(rows * top), side="right").astype(jnp.int32)
    grid = items.reshape(top, rows).T
    grid = grid[jax.random.permutation(jax.random.fold_in(own, 1), rows)]
    offset_by = jax.random.randint(jax.random.fold_in(own, 2), (rows, 1), 0, top)
    return jnp.take_along_axis(grid, (jnp.arange(top)[None, :] + offset_by) % top, axis=1)


def shares(number_of, total, limit, lean, full):
    portions = [(1 << 20) // math.isqrt(grade ** lean) + 1 for grade in range(1, number_of + 1)]
    largest = limit if full else min(limit, max(-(-total // number_of), total * portions[0] // sum(portions)))
    least = 1 if total - largest >= number_of - 1 else 0
    counts, surplus = [largest] + [least] * (number_of - 1), total - largest - least * (number_of - 1)
    while surplus > 0:
        movable = [i for i in range(1, number_of) if counts[i] < largest] or [i for i in range(1, number_of) if counts[i] < limit]
        mass, remaining = sum([portions[i] for i in movable]), surplus
        for i in movable:
            more = min(limit - counts[i], max(1, remaining * portions[i] // mass), surplus)
            counts[i] = counts[i] + more
            surplus = surplus - more
    return np.array(counts)


def scatter_about(stream_key, dims, deviation, reach, split=(), kind=jnp.bfloat16):
    gain = levels(stream_key, dims, split, -0.22, 0.18) if split else 1.0
    result = jax.random.normal(stream_key, dims, jnp.float32) * deviation * gain
    return jnp.minimum(jnp.maximum(result, -reach), reach).astype(kind)


def setup_inputs(seed: int = 0) -> dict:
    seeds = jax.random.split(jax.random.key(seed), 10)
    initial_thermal_state = scatter_about(seeds[0], (64, OCTANT_NUMBER), 1.0, 6.0, ((1, 128),), jnp.float32)
    baseline_diffusivity = jnp.clip(jnp.exp(math.log(3.0) - 2.3025851 * jax.random.uniform(seeds[1], (64, OCTANT_NUMBER), jnp.float32) ** levels(seeds[1], (64, OCTANT_NUMBER), ((1, 128),), -0.2, 0.2)), 0.3, 3.0)
    thermal_storage = jnp.clip(jnp.exp(math.log(4.0) - 2.0794415 * jax.random.uniform(seeds[2], (64, OCTANT_NUMBER), jnp.float32) ** levels(seeds[2], (64, OCTANT_NUMBER), ((1, 128),), -0.2, 0.2)), 0.5, 4.0)
    refinement_depth = place_ends(jax.random.randint(seeds[3], (OCTANT_NUMBER,), 0, 3), jax.random.fold_in(seeds[3], 1), 0, 2).astype(jnp.int32)
    interface_voxel_table = place_ends(jax.random.randint(seeds[4], (OWNERS, OWNERS, SLOTS), 0, 64 * BLK_DEV), jax.random.fold_in(seeds[4], 1), 0, (64 * BLK_DEV) - 1).astype(jnp.int32)
    interface_weighting = draw_interface_weighting(jax.random.fold_in(seeds[9], 71), 0)
    laser_energy_deposits = jnp.clip(1.0 * jax.random.uniform(seeds[6], (STEPS, POINTS, ROW_W), jnp.float32) ** levels(seeds[6], (STEPS, POINTS, ROW_W), ((1, 128),), -0.2, 0.2), 0.0, 1.0)
    laser_spot_holder_keys = jax.random.split(jax.random.fold_in(seeds[7], 1), STEPS * POINTS // PTS_DEV)
    laser_spot_holder_turns = jax.random.permutation(jax.random.fold_in(seeds[7], 3), STEPS * POINTS // PTS_DEV)
    laser_spot_holder = jax.vmap(lambda own, number: routed_block(jax.random.fold_in(seeds[7], 2), own, number, PTS_DEV, OWNERS, 1, CAP, 2))(laser_spot_holder_keys, laser_spot_holder_turns).reshape((STEPS, POINTS, 1))
    laser_spot_patch = place_ends(jax.random.randint(seeds[8], (STEPS, POINTS), 0, TILES_DEV), jax.random.fold_in(seeds[8], 1), 0, TILES_DEV - 1).astype(jnp.int32)
    return dict(initial_thermal_state=initial_thermal_state, baseline_diffusivity=baseline_diffusivity, thermal_storage=thermal_storage, refinement_depth=refinement_depth, interface_voxel_table=interface_voxel_table, interface_weighting=interface_weighting, laser_energy_deposits=laser_energy_deposits, laser_spot_holder=laser_spot_holder, laser_spot_patch=laser_spot_patch)


def cond_links(diffuse_warmth, spacing):
    grid_cube = diffuse_warmth.reshape(4, 4, 4, -1)
    first_pairs = spacing * 0.5 * (grid_cube[1:] + grid_cube[:-1])
    second_pairs = spacing * 0.5 * (grid_cube[:, 1:] + grid_cube[:, :-1])
    third_pairs = spacing * 0.5 * (grid_cube[:, :, 1:] + grid_cube[:, :, :-1])
    return first_pairs, second_pairs, third_pairs


def inside_energy_current(values, interface_couplings):
    grid_cube = values.reshape(4, 4, 4, -1)
    flux_one = interface_couplings[0] * (grid_cube[1:] - grid_cube[:-1])
    flux_two = interface_couplings[1] * (grid_cube[:, 1:] - grid_cube[:, :-1])
    flux_three = interface_couplings[2] * (grid_cube[:, :, 1:] - grid_cube[:, :, :-1])
    zero_pad = (0, 0)
    balance = jnp.pad(flux_one, ((1, 0), zero_pad, zero_pad, zero_pad)) - jnp.pad(flux_one, ((0, 1), zero_pad, zero_pad, zero_pad))
    balance = balance + jnp.pad(flux_two, (zero_pad, (1, 0), zero_pad, zero_pad)) - jnp.pad(flux_two, (zero_pad, (0, 1), zero_pad, zero_pad))
    balance = balance + jnp.pad(flux_three, (zero_pad, zero_pad, (1, 0), zero_pad)) - jnp.pad(flux_three, (zero_pad, zero_pad, (0, 1), zero_pad))
    return balance.reshape(values.shape)


def interface_energy_current(values, home_voxel_position, neighbor_position, interface_diffusivity):
    flat_vals = values.reshape(-1)
    flux_vals = interface_diffusivity * (flat_vals[home_voxel_position] - flat_vals[neighbor_position])
    return jnp.zeros_like(flat_vals).at[home_voxel_position.reshape(-1)].add(flux_vals.reshape(-1)).reshape(values.shape)


def reference(initial_thermal_state, baseline_diffusivity, thermal_storage, refinement_depth, interface_voxel_table, interface_weighting, laser_energy_deposits, laser_spot_holder, laser_spot_patch):
    owner_ids = jnp.arange(OWNERS, dtype=jnp.int32)
    home_voxel_position = (interface_voxel_table // BLK_DEV) * OCTANT_NUMBER + owner_ids[:, None, None] * BLK_DEV + interface_voxel_table % BLK_DEV
    mirror = jnp.transpose(interface_voxel_table, (1, 0, 2))
    neighbor_position = (mirror // BLK_DEV) * OCTANT_NUMBER + owner_ids[None, :, None] * BLK_DEV + mirror % BLK_DEV
    spacing = 0.5 ** refinement_depth.astype(jnp.float32)
    heat_mass = thermal_storage * spacing ** 3
    equation_misfit = jnp.zeros_like(initial_thermal_state)
    for step_num in range(STEPS):
        tile_index = laser_spot_holder[step_num, :, 0] * TILES_DEV + laser_spot_patch[step_num]
        tile_heat = jax.ops.segment_sum(laser_energy_deposits[step_num], tile_index, num_segments=TILES_DEV * OWNERS)
        energy_input = jnp.transpose(tile_heat.reshape(-1, 4, 64), (2, 0, 1)).reshape(64, OCTANT_NUMBER)
        diffuse_warmth = baseline_diffusivity * (1.0 + 0.5 * jnp.tanh(initial_thermal_state))
        interface_couplings = cond_links(diffuse_warmth, spacing)
        flat_k = diffuse_warmth.reshape(-1)
        interface_diffusivity = interface_weighting * 0.5 * (flat_k[home_voxel_position] + flat_k[neighbor_position])
        conjugate_gradient_loop = initial_thermal_state
        equation_misfit = energy_input - (inside_energy_current(initial_thermal_state, interface_couplings) + interface_energy_current(initial_thermal_state, home_voxel_position, neighbor_position, interface_diffusivity))
        direction = equation_misfit
        res_norm = jnp.sum(equation_misfit * equation_misfit)
        for turn_index in range(ITERS):
            applied = heat_mass * direction + inside_energy_current(direction, interface_couplings) + interface_energy_current(direction, home_voxel_position, neighbor_position, interface_diffusivity)
            step_size = res_norm / jnp.sum(direction * applied)
            conjugate_gradient_loop = conjugate_gradient_loop + step_size * direction
            equation_misfit = equation_misfit - step_size * applied
            next_norm = jnp.sum(equation_misfit * equation_misfit)
            direction = equation_misfit + (next_norm / res_norm) * direction
            res_norm = next_norm
        initial_thermal_state = conjugate_gradient_loop
    return initial_thermal_state, equation_misfit
```

```python
import jax
import jax.numpy as jnp
from jax import lax
from jax.experimental import pallas as pl
from jax.experimental.pallas import tpu as pltpu
from jax.sharding import PartitionSpec as P

MESH = pl.DeviceIdType.MESH

CAP = 8
ITERS = 4


def cond_links(diffuse_warmth, spacing):
    grid_cube = diffuse_warmth.reshape(4, 4, 4, -1)
    first_pairs = spacing * 0.5 * (grid_cube[1:] + grid_cube[:-1])
    second_pairs = spacing * 0.5 * (grid_cube[:, 1:] + grid_cube[:, :-1])
    third_pairs = spacing * 0.5 * (grid_cube[:, :, 1:] + grid_cube[:, :, :-1])
    return (first_pairs, second_pairs, third_pairs)


def inside_energy_current(values, interface_couplings):
    grid_cube = values.reshape(4, 4, 4, -1)
    flux_one = interface_couplings[0] * (grid_cube[1:] - grid_cube[:-1])
    flux_two = interface_couplings[1] * (grid_cube[:, 1:] - grid_cube[:, :-1])
    flux_three = interface_couplings[2] * (grid_cube[:, :, 1:] - grid_cube[:, :, :-1])
    zero_pad = (0, 0)
    balance = jnp.pad(flux_one, ((1, 0), zero_pad, zero_pad, zero_pad)) - jnp.pad(
        flux_one, ((0, 1), zero_pad, zero_pad, zero_pad)
    )
    balance = (
        balance
        + jnp.pad(flux_two, (zero_pad, (1, 0), zero_pad, zero_pad))
        - jnp.pad(flux_two, (zero_pad, (0, 1), zero_pad, zero_pad))
    )
    balance = (
        balance
        + jnp.pad(flux_three, (zero_pad, zero_pad, (1, 0), zero_pad))
        - jnp.pad(flux_three, (zero_pad, zero_pad, (0, 1), zero_pad))
    )
    return balance.reshape(values.shape)


def interface_energy_current(values, voxel_lattice, interface_diffusivity, own_vals, peer_vals):
    flux_vals = interface_diffusivity * (own_vals - peer_vals)
    flat_zero = jnp.zeros((values.size,), jnp.float32)
    return flat_zero.at[voxel_lattice.reshape(-1)].add(flux_vals.reshape(-1)).reshape(values.shape)


def apply_operator(values, heat_mass, interface_couplings, voxel_lattice, interface_diffusivity):
    own_vals = values.reshape(-1)[voxel_lattice]
    peer_vals = lax.all_to_all(own_vals, ("bx", "by"), split_axis=0, concat_axis=0, tiled=True)
    return (
        heat_mass * values
        + inside_energy_current(values, interface_couplings)
        + interface_energy_current(
            values, voxel_lattice, interface_diffusivity, own_vals, peer_vals
        )
    )


def sum_kernel(x_ref, lane_ref, o_ref, snd, rcv, ssem, rsem):
    bx, by = lax.axis_index("bx"), lax.axis_index("by")
    nx, ny = lax.axis_size("bx"), lax.axis_size("by")
    n = nx * ny
    me = bx * ny + by
    b = pltpu.get_barrier_semaphore()

    def greet(i, c):
        p = lax.rem(me + i, n)
        pl.semaphore_signal(b, inc=1, device_id=(p // ny, lax.rem(p, ny)), device_id_type=MESH)
        return c

    lax.fori_loop(1, n, greet, 0)
    x = jnp.take_along_axis(x_ref[...], lane_ref[...], axis=1)
    snd[...] = jnp.sum(x, axis=0, keepdims=True)
    rcv[pl.ds(me, 1)] = snd[...]
    pl.semaphore_wait(b, n - 1)

    def send(i, c):
        p = lax.rem(me + i, n)
        pltpu.make_async_remote_copy(
            src_ref=snd.at[pl.ds(0, 1)], dst_ref=rcv.at[pl.ds(me, 1)], send_sem=ssem, recv_sem=rsem,
            device_id=(p // ny, lax.rem(p, ny)), device_id_type=MESH,
        ).start()
        return c

    lax.fori_loop(1, n, send, 0)
    p = lax.rem(me + 1, n)
    pltpu.make_async_remote_copy(
        src_ref=rcv.at[pl.ds(0, n - 1)], dst_ref=rcv.at[pl.ds(0, n - 1)], send_sem=ssem, recv_sem=rsem,
        device_id=(p // ny, lax.rem(p, ny)), device_id_type=MESH,
    ).wait()
    o_ref[...] = jnp.broadcast_to(jnp.sum(rcv[...]), (8, 128))


def total(value):
    x = jnp.zeros((8, 128), jnp.float32).at[0, 0].set(value)
    lanes = lax.broadcasted_iota(jnp.int32, (8, 128), 1)
    n = lax.axis_size(("bx", "by"))
    return pl.pallas_call(
        sum_kernel,
        out_shape=jax.ShapeDtypeStruct((8, 128), jnp.float32),
        in_specs=[pl.BlockSpec(memory_space=pltpu.VMEM)] * 2,
        out_specs=pl.BlockSpec(memory_space=pltpu.VMEM),
        scratch_shapes=[
            pltpu.VMEM((1, 128), jnp.float32),
            pltpu.VMEM((n, 128), jnp.float32),
            pltpu.SemaphoreType.DMA,
            pltpu.SemaphoreType.DMA,
        ],
        compiler_params=pltpu.CompilerParams(collective_id=0, has_side_effects=True),
    )(x, lanes)[0, 0]


def squares(values):
    return total(jnp.sum(values * values))


def shards(
    initial_thermal_state,
    baseline_diffusivity,
    thermal_storage,
    refinement_depth,
    interface_voxel_table,
    interface_weighting,
    laser_energy_deposits,
    laser_spot_holder,
    laser_spot_patch,
):
    owner_count = lax.axis_size(("bx", "by"))
    voxel_lattice = interface_voxel_table[0]
    areas = interface_weighting[0]
    patch_number = initial_thermal_state.shape[1] // 4
    step_count = laser_energy_deposits.shape[0]
    row_width = laser_energy_deposits.shape[2]
    spacing = 0.5 ** refinement_depth.astype(jnp.float32)
    heat_mass = thermal_storage * spacing**3

    def bucket(owners, tiles, row_block):
        matches = (owners[:, None] == jnp.arange(owner_count, dtype=jnp.int32)[None, :]).astype(
            jnp.int32
        )
        slot_rank = jnp.sum((jnp.cumsum(matches, 0) - 1) * matches, 1)
        slot_dest = owners * CAP + slot_rank
        sent_rows = (
            jnp.zeros((owner_count * CAP, row_width), jnp.float32).at[slot_dest].set(row_block)
        )
        sent_ids = (
            jnp.full((owner_count * CAP,), -1.0, jnp.float32)
            .at[slot_dest]
            .set(tiles.astype(jnp.float32))
        )
        return (sent_rows.reshape(owner_count, CAP, row_width), sent_ids.reshape(owner_count, CAP))

    sent_rows, sent_ids = jax.vmap(bucket)(
        laser_spot_holder[:, :, 0], laser_spot_patch, laser_energy_deposits
    )
    got_rows, got_ids = (
        lax.all_to_all(sent_rows, ("bx", "by"), split_axis=1, concat_axis=1, tiled=True),
        lax.all_to_all(sent_ids, ("bx", "by"), split_axis=1, concat_axis=1, tiled=True),
    )
    got_rows = got_rows.reshape(step_count, -1, row_width)
    got_ids = got_ids.reshape(step_count, -1)
    tile_iota = jnp.arange(patch_number, dtype=jnp.float32)
    equation_misfit = jnp.zeros_like(initial_thermal_state)
    matches = (got_ids[0][None, :] == tile_iota[:, None]).astype(jnp.float32)
    tile_heat = jnp.dot(
        matches, got_rows[0], precision=lax.Precision.HIGHEST, preferred_element_type=jnp.float32
    )
    energy_input = jnp.transpose(tile_heat.reshape(patch_number, 4, 64), (2, 0, 1)).reshape(
        64, patch_number * 4
    )
    diffuse_warmth = baseline_diffusivity * (1.0 + 0.5 * jnp.tanh(initial_thermal_state))
    interface_couplings = cond_links(diffuse_warmth, spacing)
    own_k = diffuse_warmth.reshape(-1)[voxel_lattice]
    home_thermal_state = initial_thermal_state.reshape(-1)[voxel_lattice]
    peer_k = lax.all_to_all(own_k, ("bx", "by"), split_axis=0, concat_axis=0, tiled=True)
    neighbor_thermal_state = lax.all_to_all(
        home_thermal_state, ("bx", "by"), split_axis=0, concat_axis=0, tiled=True
    )
    interface_diffusivity = areas * 0.5 * (own_k + peer_k)
    equation_misfit = energy_input - (
        inside_energy_current(initial_thermal_state, interface_couplings)
        + interface_energy_current(
            initial_thermal_state,
            voxel_lattice,
            interface_diffusivity,
            home_thermal_state,
            neighbor_thermal_state,
        )
    )
    conjugate_gradient_loop = initial_thermal_state

    def one_turn(turn_index, carry):
        conjugate_gradient_loop, equation_misfit, direction, res_norm = carry
        applied = apply_operator(
            direction, heat_mass, interface_couplings, voxel_lattice, interface_diffusivity
        )
        step_size = res_norm / total(jnp.sum(direction * applied))
        conjugate_gradient_loop = conjugate_gradient_loop + step_size * direction
        equation_misfit = equation_misfit - step_size * applied
        next_norm = squares(equation_misfit)
        direction = equation_misfit + next_norm / res_norm * direction
        return (conjugate_gradient_loop, equation_misfit, direction, next_norm)

    start_norm = squares(equation_misfit)
    conjugate_gradient_loop, equation_misfit, direction, start_norm = lax.fori_loop(
        0, ITERS, one_turn, (conjugate_gradient_loop, equation_misfit, equation_misfit, start_norm)
    )
    return (conjugate_gradient_loop, equation_misfit)


def solution(mesh):
    return jax.shard_map(
        shards,
        mesh=mesh,
        in_specs=(
            P(None, ("bx", "by")),
            P(None, ("bx", "by")),
            P(None, ("bx", "by")),
            P(("bx", "by")),
            P(("bx", "by"), None, None),
            P(("bx", "by"), None, None),
            P(None, ("bx", "by"), None),
            P(None, ("bx", "by"), None),
            P(None, ("bx", "by")),
        ),
        out_specs=(P(None, ("bx", "by")), P(None, ("bx", "by"))),
        check_vma=False,
    )
```

```python
import functools

import jax
import jax.numpy as jnp
from jax import lax
from jax.experimental import pallas as pl
from jax.experimental.pallas import tpu as pltpu
from jax.sharding import PartitionSpec as P

CAP = 8
ITERS = 4
MESH = pl.DeviceIdType.MESH
F32, BF16, I32 = jnp.float32, jnp.bfloat16, jnp.int32
ROUNDS = 6


def cond_links(diffuse_warmth, spacing):
    grid_cube = diffuse_warmth.reshape(4, 4, 4, -1)
    first_pairs = spacing * 0.5 * (grid_cube[1:] + grid_cube[:-1])
    second_pairs = spacing * 0.5 * (grid_cube[:, 1:] + grid_cube[:, :-1])
    third_pairs = spacing * 0.5 * (grid_cube[:, :, 1:] + grid_cube[:, :, :-1])
    return (first_pairs, second_pairs, third_pairs)


def inside_energy_current(values, interface_couplings):
    grid_cube = values.reshape(4, 4, 4, -1)
    flux_one = interface_couplings[0] * (grid_cube[1:] - grid_cube[:-1])
    flux_two = interface_couplings[1] * (grid_cube[:, 1:] - grid_cube[:, :-1])
    flux_three = interface_couplings[2] * (grid_cube[:, :, 1:] - grid_cube[:, :, :-1])
    zero_pad = (0, 0)
    balance = jnp.pad(flux_one, ((1, 0), zero_pad, zero_pad, zero_pad)) - jnp.pad(
        flux_one, ((0, 1), zero_pad, zero_pad, zero_pad)
    )
    balance = (
        balance
        + jnp.pad(flux_two, (zero_pad, (1, 0), zero_pad, zero_pad))
        - jnp.pad(flux_two, (zero_pad, (0, 1), zero_pad, zero_pad))
    )
    balance = (
        balance
        + jnp.pad(flux_three, (zero_pad, zero_pad, (1, 0), zero_pad))
        - jnp.pad(flux_three, (zero_pad, zero_pad, (0, 1), zero_pad))
    )
    return balance.reshape(values.shape)


def interface_energy_current(values, voxel_lattice, interface_diffusivity, own_vals, peer_vals):
    flux_vals = interface_diffusivity * (own_vals - peer_vals)
    flat_zero = jnp.zeros((values.size,), jnp.float32)
    return flat_zero.at[voxel_lattice.reshape(-1)].add(flux_vals.reshape(-1)).reshape(values.shape)


def apply_operator(values, heat_mass, interface_couplings, voxel_lattice, interface_diffusivity):
    own_vals = values.reshape(-1)[voxel_lattice]
    peer_vals = lax.all_to_all(own_vals, ("bx", "by"), split_axis=0, concat_axis=0, tiled=True)
    return (
        heat_mass * values
        + inside_energy_current(values, interface_couplings)
        + interface_energy_current(
            values, voxel_lattice, interface_diffusivity, own_vals, peer_vals
        )
    )


def squares(values):
    return lax.psum(jnp.sum(values * values), ("bx", "by"))


def general(
    initial_thermal_state,
    baseline_diffusivity,
    thermal_storage,
    refinement_depth,
    interface_voxel_table,
    interface_weighting,
    laser_energy_deposits,
    laser_spot_holder,
    laser_spot_patch,
):
    owner_count = lax.axis_size(("bx", "by"))
    voxel_lattice = interface_voxel_table[0]
    areas = interface_weighting[0]
    patch_number = initial_thermal_state.shape[1] // 4
    step_count = laser_energy_deposits.shape[0]
    row_width = laser_energy_deposits.shape[2]
    spacing = 0.5 ** refinement_depth.astype(jnp.float32)
    heat_mass = thermal_storage * spacing**3

    def bucket(owners, tiles, row_block):
        matches = (owners[:, None] == jnp.arange(owner_count, dtype=jnp.int32)[None, :]).astype(
            jnp.int32
        )
        slot_rank = jnp.sum((jnp.cumsum(matches, 0) - 1) * matches, 1)
        slot_dest = owners * CAP + slot_rank
        sent_rows = (
            jnp.zeros((owner_count * CAP, row_width), jnp.float32).at[slot_dest].set(row_block)
        )
        sent_ids = (
            jnp.full((owner_count * CAP,), -1.0, jnp.float32)
            .at[slot_dest]
            .set(tiles.astype(jnp.float32))
        )
        return (sent_rows.reshape(owner_count, CAP, row_width), sent_ids.reshape(owner_count, CAP))

    sent_rows, sent_ids = jax.vmap(bucket)(
        laser_spot_holder[:, :, 0], laser_spot_patch, laser_energy_deposits
    )
    got_rows, got_ids = (
        lax.all_to_all(sent_rows, ("bx", "by"), split_axis=1, concat_axis=1, tiled=True),
        lax.all_to_all(sent_ids, ("bx", "by"), split_axis=1, concat_axis=1, tiled=True),
    )
    got_rows = got_rows.reshape(step_count, -1, row_width)
    got_ids = got_ids.reshape(step_count, -1)
    tile_iota = jnp.arange(patch_number, dtype=jnp.float32)
    equation_misfit = jnp.zeros_like(initial_thermal_state)
    matches = (got_ids[0][None, :] == tile_iota[:, None]).astype(jnp.float32)
    tile_heat = jnp.dot(
        matches, got_rows[0], precision=lax.Precision.HIGHEST, preferred_element_type=jnp.float32
    )
    energy_input = jnp.transpose(tile_heat.reshape(patch_number, 4, 64), (2, 0, 1)).reshape(
        64, patch_number * 4
    )
    diffuse_warmth = baseline_diffusivity * (1.0 + 0.5 * jnp.tanh(initial_thermal_state))
    interface_couplings = cond_links(diffuse_warmth, spacing)
    own_k = diffuse_warmth.reshape(-1)[voxel_lattice]
    home_thermal_state = initial_thermal_state.reshape(-1)[voxel_lattice]
    peer_k = lax.all_to_all(own_k, ("bx", "by"), split_axis=0, concat_axis=0, tiled=True)
    neighbor_thermal_state = lax.all_to_all(
        home_thermal_state, ("bx", "by"), split_axis=0, concat_axis=0, tiled=True
    )
    interface_diffusivity = areas * 0.5 * (own_k + peer_k)
    equation_misfit = energy_input - (
        inside_energy_current(initial_thermal_state, interface_couplings)
        + interface_energy_current(
            initial_thermal_state,
            voxel_lattice,
            interface_diffusivity,
            home_thermal_state,
            neighbor_thermal_state,
        )
    )
    conjugate_gradient_loop = initial_thermal_state

    def one_turn(turn_index, carry):
        conjugate_gradient_loop, equation_misfit, direction, res_norm = carry
        applied = apply_operator(
            direction, heat_mass, interface_couplings, voxel_lattice, interface_diffusivity
        )
        step_size = res_norm / lax.psum(jnp.sum(direction * applied), ("bx", "by"))
        conjugate_gradient_loop = conjugate_gradient_loop + step_size * direction
        equation_misfit = equation_misfit - step_size * applied
        next_norm = squares(equation_misfit)
        direction = equation_misfit + next_norm / res_norm * direction
        return (conjugate_gradient_loop, equation_misfit, direction, next_norm)

    start_norm = squares(equation_misfit)
    conjugate_gradient_loop, equation_misfit, direction, start_norm = lax.fori_loop(
        0, ITERS, one_turn, (conjugate_gradient_loop, equation_misfit, equation_misfit, start_norm)
    )
    return (conjugate_gradient_loop, equation_misfit)


def lanes_of(x, idx):
    return jnp.take_along_axis(x, idx, axis=1, mode="promise_in_bounds")


def thirds(x):
    a = x.astype(BF16)
    rest = x - a.astype(F32)
    b = rest.astype(BF16)
    c = (rest - b.astype(F32)).astype(BF16)
    return a, b, c


def iota(shape, dim):
    return lax.broadcasted_iota(I32, shape, dim)


def dot_nt(a, b):
    return lax.dot_general(a, b, (((1,), (1,)), ((), ())), preferred_element_type=F32)


def dot_nn(a, b):
    return jnp.dot(a, b, preferred_element_type=F32)


def peers():
    bx, by = lax.axis_index("bx"), lax.axis_index("by")
    offs = []
    for dc in range(2):
        for dy in range(4):
            for dx in range(4):
                for dz in range(4):
                    if (dc, dy, dx, dz) != (0, 0, 0, 0):
                        hops = min(dy, 4 - dy) + min(dx, 4 - dx) + min(dz, 4 - dz)
                        offs.append((-hops, dc, dy, dx, dz))
    offs.sort()
    y, core, x, z = bx // 2, lax.rem(bx, 2), by // 4, lax.rem(by, 4)
    for _, dc, dy, dx, dz in offs:
        px = lax.rem(y + dy, 4) * 2 + lax.rem(core + dc, 2)
        py = lax.rem(x + dx, 4) * 4 + lax.rem(z + dz, 4)
        yield px, py


def step_kernel(
    temp_hbm, base_hbm, store_hbm, level_hbm, face_hbm, area_hbm, rows_hbm, owner_hbm, tile_hbm,
    x_out, r_out, flag_out,
    in_t, in_b, in_s, level, face, area, rows, owner, tile,
    xf, kf, mf, gx, gy, gz, ra, rb, wf, sf, pf, nat, en,
    ohs, ohl, celltab, lanetab, srcrow, srclane, rowid, slane, slots, slots2, msgs,
    ro, rp, so, sp, gface, heat, oht,
    snd, rcv, lsnd, lrcv,
    in_sem, ssem, rsem, lssem, lrsem, out_sem,
):
    bx, by = lax.axis_index("bx"), lax.axis_index("by")
    me = bx * 16 + by
    barrier = pltpu.get_barrier_semaphore()
    for px, py in peers():
        pl.semaphore_signal(barrier, inc=1, device_id=(px, py), device_id_type=MESH)

    loads = [
        pltpu.make_async_copy(src, dst, in_sem.at[i])
        for i, (src, dst) in enumerate(
            [(owner_hbm, owner), (tile_hbm, tile), (rows_hbm, rows), (face_hbm, face), (area_hbm, area), (level_hbm, level),
             (temp_hbm, in_t), (base_hbm, in_b), (store_hbm, in_s)]
        )
    ]
    for c in loads:
        c.start()

    for c in loads[:3]:
        c.wait()
    own = owner[...]
    match = iota((128, 256), 0) == own
    upto = (iota((256, 256), 0) <= iota((256, 256), 1)).astype(F32).astype(BF16)
    before = dot_nn(match.astype(F32).astype(BF16), upto) - 1.0
    rank = jnp.sum(jnp.where(match, before, 0.0), axis=0, keepdims=True)
    dest = own * CAP + rank.astype(I32)
    place = (iota((1024, 256), 0) == dest).astype(F32).astype(BF16)
    pieces = thirds(rows[...])
    put = (dot_nn(place, pieces[0]) + dot_nn(place, pieces[1])) + dot_nn(place, pieces[2])
    lsnd[...] = put.reshape(128, 8, 256)
    num = tile[...] + 1
    is_rank = iota((8, 256), 0) == rank.astype(I32)
    high = jnp.where(is_rank, num >> 5, 0).astype(F32)
    low = jnp.where(is_rank, num & 31, 0).astype(F32)
    hl = jnp.concatenate([high, low], axis=0).astype(BF16)
    ids = dot_nt(hl, match.astype(F32).astype(BF16))
    ids = ids[0:8] * 32.0 + ids[8:16] - 1.0

    for c in loads[3:6]:
        c.wait()
    fc = face[...]
    bt = (fc & 4095) >> 7
    for i in range(32):
        ohs[pl.ds(32 * i, 32), :] = (iota((32, 128), 0) == bt[i : i + 1]).astype(F32).astype(BF16)
    tri = (iota((128, 128), 0) <= iota((128, 128), 1)).astype(F32).astype(BF16)
    ones = jnp.ones((128, 128), BF16)
    run = jnp.zeros((32, 128), F32)
    ranks = []
    for i in range(32):
        oh = ohs[pl.ds(32 * i, 32), :]
        pre = dot_nn(oh, tri)
        ranks.append(jnp.sum(oh.astype(F32) * (pre + run - 1.0), axis=0, keepdims=True))
        run = run + dot_nn(oh, ones)
    rank = jnp.concatenate(ranks, axis=0).astype(I32)
    over = jnp.max(jnp.max((rank >= 256).astype(F32), axis=0, keepdims=True), axis=1, keepdims=True)
    rid = (rank >> 7) * 32 + bt
    rowid[...] = rid
    slane[...] = rank & 127
    cellv = (fc >> 12).astype(F32)
    lanev = (fc & 127).astype(F32)
    lane_f = iota((1, 128), 1).astype(F32)
    acc = jnp.zeros((256, 128), F32)
    for i in range(32):
        hit = iota((64, 128), 0) == rid[i : i + 1]
        a = jnp.concatenate(
            [
                jnp.where(hit, F32(i + 1), 0.0),
                jnp.where(hit, lane_f, 0.0),
                jnp.where(hit, cellv[i : i + 1], 0.0),
                jnp.where(hit, lanev[i : i + 1], 0.0),
            ],
            axis=0,
        ).astype(BF16)
        b = (iota((128, 128), 0) == slane[i : i + 1, :]).astype(F32).astype(BF16)
        acc = acc + dot_nt(a, b)
    tab = acc.astype(I32)
    filled = tab[0:64] > 0
    srcrow[...] = tab[0:64] - 1
    srclane[...] = tab[64:128]
    celltab[...] = jnp.where(filled, tab[128:192], -1)
    lanetab[...] = tab[192:256]

    def lane_hot(b, c):
        for h in range(2):
            row = lanetab[pl.ds(b + 32 * h, 1), :]
            ohl[pl.ds(b, 1), :, pl.ds(128 * h, 128)] = (
                (iota((128, 128), 0) == row).astype(F32).astype(BF16).reshape(1, 128, 128)
            )
        return c

    lax.fori_loop(0, 32, lane_hot, 0)

    for c in loads[6:]:
        c.wait()

    def prepare(k, c):
        lv = level[pl.ds(8 * k, 8), :]
        spacing = jnp.where(lv == 0, 1.0, jnp.where(lv == 1, 0.5, 0.25)).astype(F32)
        cube = spacing * spacing * spacing
        half = spacing * 0.5
        at = pl.ds(8 * k, 8)
        kv = {}
        for c in range(64):
            i, j, l = c // 16, (c // 4) % 4, c % 4
            where = pl.ds((c // 8) * 256 + c % 8 + 64 * k, 8, stride=8)
            t = in_t[where, :]
            kc = in_b[where, :] * (1.0 + 0.5 * jnp.tanh(t))
            xf[c, at, :] = t
            kf[c, at, :] = kc
            mf[c, at, :] = in_s[where, :] * cube
            kv[c] = kc
            if i:
                gx[c - 16, at, :] = half * (kc + kv.pop(c - 16))
            if j:
                gy[(i * 3 + j - 1) * 4 + l, at, :] = half * (kc + kv[c - 4])
            if l:
                gz[(i * 4 + j) * 3 + l - 1, at, :] = half * (kc + kv[c - 1])
        return 0

    lax.fori_loop(0, 4, prepare, 0)

    def gather(field, out):
        def group(k, c):
            at, at2 = pl.ds(8 * k, 8), pl.ds(32 + 8 * k, 8)
            l0, l1, c0, c1 = lanetab[at, :], lanetab[at2, :], celltab[at, :], celltab[at2, :]
            a0 = jnp.zeros((8, 128), F32)
            a1 = jnp.zeros((8, 128), F32)
            for cell in range(64):
                v = field[cell, at, :]
                a0 = jnp.where(c0 == cell, lanes_of(v, l0), a0)
                a1 = jnp.where(c1 == cell, lanes_of(v, l1), a1)
            out[at, :] = a0
            out[at2, :] = a1
            return c

        lax.fori_loop(0, 4, group, 0)

    def to_entries(src):
        outs = []
        for g in range(4):
            ri, la = rowid[8 * g : 8 * g + 8, :], slane[8 * g : 8 * g + 8, :]
            a = jnp.zeros((8, 128), F32)
            for t in range(64):
                row = jnp.broadcast_to(src[t : t + 1, :], (8, 128))
                a = jnp.where(ri == t, lanes_of(row, la), a)
            outs.append(a)
        return jnp.concatenate(outs, axis=0)

    def to_slots(src, out):
        for g in range(8):
            ri, la = srcrow[8 * g : 8 * g + 8, :], srclane[8 * g : 8 * g + 8, :]
            a = jnp.zeros((8, 128), F32)
            for t in range(32):
                row = jnp.broadcast_to(src[t : t + 1, :], (8, 128))
                a = jnp.where(ri == t, lanes_of(row, la), a)
            out[8 * g : 8 * g + 8, :] = a

    def scatter(flux):
        def one(b, c):
            parts = [[], [], []]
            for h in range(2):
                row = flux[pl.ds(b + 32 * h, 1), :]
                hit = iota((64, 128), 0) == celltab[pl.ds(b + 32 * h, 1), :]
                p0 = row.astype(BF16).astype(F32)
                p1 = (row - p0).astype(BF16).astype(F32)
                p2 = row - p0 - p1
                for q, p in enumerate((p0, p1, p2)):
                    parts[q].append(jnp.where(hit, p, 0.0))
            a = jnp.concatenate([jnp.concatenate(p, axis=1) for p in parts], axis=0).astype(BF16)
            o = dot_nt(a, ohl[b])
            nat[pl.ds(64 * b, 64), :] = (o[0:64] + o[64:128]) + o[128:192]
            return c

        lax.fori_loop(0, 32, one, 0, unroll=4)

    def stencil(k, load, emit, mass):
        at = pl.ds(8 * k, 8)
        v, acc = {}, {}
        for c in range(64):
            i, j, l = c // 16, (c // 4) % 4, c % 4
            v[c] = load(c)
            a = mf[c, at, :] * v[c] if mass else jnp.zeros((8, 128), F32)
            if l:
                f = gz[(i * 4 + j) * 3 + l - 1, at, :] * (v[c] - v[c - 1])
                a, acc[c - 1] = a + f, acc[c - 1] - f
            if j:
                f = gy[(i * 3 + j - 1) * 4 + l, at, :] * (v[c] - v[c - 4])
                a, acc[c - 4] = a + f, acc[c - 4] - f
            if i:
                f = gx[c - 16, at, :] * (v[c] - v.pop(c - 16))
                a = a + f
                emit(c - 16, acc.pop(c - 16) - f)
            acc[c] = a
        for c in range(48, 64):
            emit(c, acc[c])

    def send(r, feats):
        n = sum(f.shape[0] for f in feats)
        full = jnp.concatenate(list(feats) + [jnp.zeros((128 - n, 128), F32)], axis=0)
        snd[r] = full.T
        rcv[r, pl.ds(me, 1), :] = snd[r, pl.ds(me, 1), :]
        for px, py in peers():
            pltpu.make_async_remote_copy(
                src_ref=snd.at[r, pl.ds(px * 16 + py, 1)], dst_ref=rcv.at[r, pl.ds(me, 1)],
                send_sem=ssem.at[r], recv_sem=rsem.at[r], device_id=(px, py), device_id_type=MESH,
            ).start()

    def all_of(r):
        return pltpu.make_async_remote_copy(
            src_ref=snd.at[r, pl.ds(0, 127)], dst_ref=rcv.at[r, pl.ds(0, 127)],
            send_sem=ssem.at[r], recv_sem=rsem.at[r],
            device_id=(lax.rem(bx + 1, 8), by), device_id_type=MESH,
        )

    def receive(r):
        all_of(r).wait_recv()
        return rcv[r].T

    def total(rows):
        return jnp.sum(rows, axis=1, keepdims=True)

    pl.semaphore_wait(barrier, 127)
    lrcv[pl.ds(me, 1)] = lsnd[pl.ds(me, 1)]

    gather(kf, slots)
    gather(xf, slots2)
    send(0, [to_entries(slots), to_entries(slots2), ids, jnp.broadcast_to(over, (8, 128))])
    for px, py in peers():
        pltpu.make_async_remote_copy(
            src_ref=lsnd.at[pl.ds(px * 16 + py, 1)], dst_ref=lrcv.at[pl.ds(me, 1)],
            send_sem=lssem, recv_sem=lrsem, device_id=(px, py), device_id_type=MESH,
        ).start()
    msgs[...] = receive(0)
    to_slots(msgs.at[pl.ds(0, 32)], gface)
    to_slots(msgs.at[pl.ds(32, 32)], rp)
    to_slots(area, ro)
    gface[...] = ro[...] * 0.5 * (slots[...] + gface[...])
    slots[...] = gface[...] * (slots2[...] - rp[...])
    scatter(slots)
    flag_out[...] = jnp.broadcast_to(jnp.max(msgs[72:80, :], axis=1, keepdims=True), (8, 128))
    tids = msgs[64:72, :].astype(I32)
    for j in range(8):
        oht[:, pl.ds(128 * j, 128)] = (iota((1024, 128), 0) == tids[j : j + 1]).astype(F32).astype(BF16)

    laser = pltpu.make_async_remote_copy(
        src_ref=lsnd.at[pl.ds(0, 127)], dst_ref=lrcv.at[pl.ds(0, 127)],
        send_sem=lssem, recv_sem=lrsem, device_id=(lax.rem(bx + 1, 8), by), device_id_type=MESH,
    )
    laser.wait_recv()
    by_rank = []
    for j in range(8):
        by_rank.append(lrcv[:, j, :])
    pieces = thirds(jnp.concatenate(by_rank, axis=0))
    for q in range(8):
        o = oht[pl.ds(128 * q, 128), :]
        h = (dot_nn(o, pieces[0]) + dot_nn(o, pieces[1])) + dot_nn(o, pieces[2])
        heat[:, pl.ds(128 * q, 128)] = h.T
    lane = iota((8, 128), 1)
    for b in range(32):
        idx = 32 * (b % 4) + (lane >> 2)
        for g in range(8):
            a = jnp.zeros((8, 128), F32)
            for q in range(4):
                v = heat[64 * q + 8 * g : 64 * q + 8 * g + 8, 128 * (b // 4) : 128 * (b // 4) + 128]
                a = jnp.where((lane & 3) == q, lanes_of(v, idx), a)
            en[64 * b + 8 * g : 64 * b + 8 * g + 8, :] = a

    def first(k, rr):
        at = pl.ds(8 * k, 8)
        total_rr = [rr]

        def emit(c, a):
            here = pl.ds(512 * k + c, 8, stride=64)
            r = en[here, :] - (a + nat[here, :])
            ra[c, at, :] = r
            total_rr[0] = total_rr[0] + r * r

        stencil(k, lambda c: xf[c, at, :], emit, False)
        return total_rr[0]

    zero = jnp.zeros((8, 128), F32)
    lax.fori_loop(0, 4, first, zero)
    gather(ra, ro)
    send(1, [to_entries(ro)])
    msgs[...] = receive(1)
    to_slots(msgs.at[pl.ds(0, 32)], rp)

    def image(rnew, load):
        slots[...] = gface[...] * (ro[...] - rp[...])
        scatter(slots)

        def group(k, sums):
            at = pl.ds(8 * k, 8)
            s = list(sums)

            def emit(c, a):
                r = rnew[c, at, :]
                w = a + nat[pl.ds(512 * k + c, 8, stride=64), :]
                wf[c, at, :] = w
                s[0] = s[0] + r * r
                s[1] = s[1] + r * w

            stencil(k, lambda c: load(k, c), emit, True)
            return tuple(s)

        rr, rw = lax.fori_loop(0, 4, group, (zero, zero))
        full = [jnp.sum(jnp.sum(v, axis=0, keepdims=True), axis=1, keepdims=True) for v in (rr, rw)]
        return [jnp.broadcast_to(v, (8, 128)) for v in full]

    rr, rw = image(ra, lambda k, c: ra[c, pl.ds(8 * k, 8), :])
    old_rr = old_alpha = None
    r_now, r_next = ra, rb
    for it in range(ITERS):
        last = it == ITERS - 1
        if last:
            send(it + 2, [rr, rw])
        else:
            gather(wf, slots)
            send(it + 2, [to_entries(slots), rr, rw])
        if it:
            def advance(k, c, it=it, beta=beta, alpha=alpha, r_old=r_old):
                at = pl.ds(8 * k, 8)
                for cell in range(64):
                    d = r_old[cell, at, :]
                    if it > 1:
                        d = d + beta * pf[cell, at, :]
                    pf[cell, at, :] = d
                    xf[cell, at, :] = xf[cell, at, :] + alpha * d
                return c

            lax.fori_loop(0, 4, advance, 0)
        msgs[...] = receive(it + 2)
        base = 0 if last else 32
        g_rr, g_rw = total(msgs[base : base + 1, :]), total(msgs[base + 8 : base + 9, :])
        if it:
            beta1 = g_rr / old_rr
            alpha1 = g_rr / (g_rw - beta1 * g_rr / old_alpha)
            beta = jnp.broadcast_to(beta1, (8, 128))
        else:
            alpha1 = g_rr / g_rw
            beta = None
        alpha = jnp.broadcast_to(alpha1, (8, 128))
        old_rr, old_alpha = g_rr, alpha1
        r_old = r_now
        if last:
            break
        to_slots(msgs.at[pl.ds(0, 32)], slots2)
        if it:
            so[...] = slots[...] + beta1 * so[...]
            sp[...] = slots2[...] + beta1 * sp[...]
        else:
            so[...] = slots[...]
            sp[...] = slots2[...]
        ro[...] = ro[...] - alpha1 * so[...]
        rp[...] = rp[...] - alpha1 * sp[...]

        def load(k, c, it=it, alpha=alpha, beta=beta, r_now=r_now, r_next=r_next):
            at = pl.ds(8 * k, 8)
            s = wf[c, at, :]
            if it:
                s = s + beta * sf[c, at, :]
            sf[c, at, :] = s
            r = r_now[c, at, :] - alpha * s
            r_next[c, at, :] = r
            return r

        rr, rw = image(r_next, load)
        r_now, r_next = r_next, r_now

    def finish(k, c):
        at = pl.ds(8 * k, 8)
        for cell in range(64):
            where = pl.ds((cell // 8) * 256 + cell % 8 + 64 * k, 8, stride=8)
            r = r_now[cell, at, :]
            d = r + beta * pf[cell, at, :]
            in_t[where, :] = xf[cell, at, :] + alpha * d
            in_b[where, :] = r - alpha * (wf[cell, at, :] + beta * sf[cell, at, :])
        return c

    lax.fori_loop(0, 4, finish, 0)
    outs = [pltpu.make_async_copy(in_t, x_out, out_sem.at[0]), pltpu.make_async_copy(in_b, r_out, out_sem.at[1])]
    for c in outs:
        c.start()
    for r in range(ROUNDS):
        all_of(r).wait_send()
    laser.wait_send()
    for c in outs:
        c.wait()


def tiled(v):
    return v.reshape(8, 8, 32, 128).transpose(0, 2, 1, 3).reshape(2048, 128)


def untiled(v):
    return v.reshape(8, 32, 8, 128).transpose(0, 2, 1, 3).reshape(64, 4096)


def vm(*shape, dtype=F32):
    return pltpu.VMEM(shape, dtype)


def shards(*args):
    temp, base, store, level, face, area, rows, owner, tile = args
    field = lambda: vm(64, 32, 128)
    part = lambda: vm(48, 32, 128)
    slot = lambda dtype=F32: vm(64, 128, dtype=dtype)
    x, r, flag = pl.pallas_call(
        step_kernel,
        out_shape=[
            jax.ShapeDtypeStruct((2048, 128), F32),
            jax.ShapeDtypeStruct((2048, 128), F32),
            jax.ShapeDtypeStruct((8, 128), F32),
        ],
        in_specs=[pl.BlockSpec(memory_space=pl.ANY)] * 9,
        out_specs=[pl.BlockSpec(memory_space=pl.ANY)] * 2 + [pl.BlockSpec(memory_space=pltpu.VMEM)],
        scratch_shapes=[
            vm(2048, 128), vm(2048, 128), vm(2048, 128),
            vm(32, 128, dtype=I32), vm(32, 128, dtype=I32), vm(32, 128), vm(256, 256),
            vm(1, 256, dtype=I32), vm(1, 256, dtype=I32),
            field(), field(), field(), part(), part(), part(),
            field(), field(), field(), field(), field(), vm(2048, 128), vm(2048, 128),
            vm(1024, 128, dtype=BF16), vm(32, 128, 256, dtype=BF16),
            slot(I32), slot(I32), slot(I32), slot(I32), vm(32, 128, dtype=I32), vm(32, 128, dtype=I32),
            slot(), slot(), vm(128, 128),
            slot(), slot(), slot(), slot(), slot(), vm(256, 1024), vm(1024, 1024, dtype=BF16),
            vm(ROUNDS, 128, 128), vm(ROUNDS, 128, 128), vm(128, 8, 256), vm(128, 8, 256),
            pltpu.SemaphoreType.DMA((9,)),
            pltpu.SemaphoreType.DMA((ROUNDS,)),
            pltpu.SemaphoreType.DMA((ROUNDS,)),
            pltpu.SemaphoreType.DMA,
            pltpu.SemaphoreType.DMA,
            pltpu.SemaphoreType.DMA((2,)),
        ],
        compiler_params=pltpu.CompilerParams(
            collective_id=0, has_side_effects=True, vmem_limit_bytes=56 * 1024 * 1024
        ),
    )(
        tiled(temp), tiled(base), tiled(store), level.reshape(32, 128),
        face[0].T, area[0].T, rows[0], owner.reshape(1, 256), tile,
    )
    return lax.cond(
        flag[0, 0] > 0.5,
        lambda: general(*args),
        lambda: (untiled(x), untiled(r)),
    )


def solution(mesh):
    return jax.shard_map(
        shards,
        mesh=mesh,
        in_specs=(
            P(None, ("bx", "by")),
            P(None, ("bx", "by")),
            P(None, ("bx", "by")),
            P(("bx", "by")),
            P(("bx", "by"), None, None),
            P(("bx", "by"), None, None),
            P(None, ("bx", "by"), None),
            P(None, ("bx", "by"), None),
            P(None, ("bx", "by")),
        ),
        out_specs=(P(None, ("bx", "by")), P(None, ("bx", "by"))),
        check_vma=False,
    )
```

```python
import functools

import jax
import jax.numpy as jnp
from jax import lax
from jax.experimental import pallas as pl
from jax.experimental.pallas import tpu as pltpu
from jax.sharding import PartitionSpec as P

CAP = 8
ITERS = 4
MESH = pl.DeviceIdType.MESH
F32, BF16, I32 = jnp.float32, jnp.bfloat16, jnp.int32
ROUNDS = 6
MEMBERS = 5


def cond_links(diffuse_warmth, spacing):
    grid_cube = diffuse_warmth.reshape(4, 4, 4, -1)
    first_pairs = spacing * 0.5 * (grid_cube[1:] + grid_cube[:-1])
    second_pairs = spacing * 0.5 * (grid_cube[:, 1:] + grid_cube[:, :-1])
    third_pairs = spacing * 0.5 * (grid_cube[:, :, 1:] + grid_cube[:, :, :-1])
    return (first_pairs, second_pairs, third_pairs)


def inside_energy_current(values, interface_couplings):
    grid_cube = values.reshape(4, 4, 4, -1)
    flux_one = interface_couplings[0] * (grid_cube[1:] - grid_cube[:-1])
    flux_two = interface_couplings[1] * (grid_cube[:, 1:] - grid_cube[:, :-1])
    flux_three = interface_couplings[2] * (grid_cube[:, :, 1:] - grid_cube[:, :, :-1])
    zero_pad = (0, 0)
    balance = jnp.pad(flux_one, ((1, 0), zero_pad, zero_pad, zero_pad)) - jnp.pad(
        flux_one, ((0, 1), zero_pad, zero_pad, zero_pad)
    )
    balance = (
        balance
        + jnp.pad(flux_two, (zero_pad, (1, 0), zero_pad, zero_pad))
        - jnp.pad(flux_two, (zero_pad, (0, 1), zero_pad, zero_pad))
    )
    balance = (
        balance
        + jnp.pad(flux_three, (zero_pad, zero_pad, (1, 0), zero_pad))
        - jnp.pad(flux_three, (zero_pad, zero_pad, (0, 1), zero_pad))
    )
    return balance.reshape(values.shape)


def interface_energy_current(values, voxel_lattice, interface_diffusivity, own_vals, peer_vals):
    flux_vals = interface_diffusivity * (own_vals - peer_vals)
    flat_zero = jnp.zeros((values.size,), jnp.float32)
    return flat_zero.at[voxel_lattice.reshape(-1)].add(flux_vals.reshape(-1)).reshape(values.shape)


def apply_operator(values, heat_mass, interface_couplings, voxel_lattice, interface_diffusivity):
    own_vals = values.reshape(-1)[voxel_lattice]
    peer_vals = lax.all_to_all(own_vals, ("bx", "by"), split_axis=0, concat_axis=0, tiled=True)
    return (
        heat_mass * values
        + inside_energy_current(values, interface_couplings)
        + interface_energy_current(
            values, voxel_lattice, interface_diffusivity, own_vals, peer_vals
        )
    )


def squares(values):
    return lax.psum(jnp.sum(values * values), ("bx", "by"))


def general(
    initial_thermal_state,
    baseline_diffusivity,
    thermal_storage,
    refinement_depth,
    interface_voxel_table,
    interface_weighting,
    laser_energy_deposits,
    laser_spot_holder,
    laser_spot_patch,
):
    owner_count = lax.axis_size(("bx", "by"))
    voxel_lattice = interface_voxel_table[0]
    areas = interface_weighting[0]
    patch_number = initial_thermal_state.shape[1] // 4
    step_count = laser_energy_deposits.shape[0]
    row_width = laser_energy_deposits.shape[2]
    spacing = 0.5 ** refinement_depth.astype(jnp.float32)
    heat_mass = thermal_storage * spacing**3

    def bucket(owners, tiles, row_block):
        matches = (owners[:, None] == jnp.arange(owner_count, dtype=jnp.int32)[None, :]).astype(
            jnp.int32
        )
        slot_rank = jnp.sum((jnp.cumsum(matches, 0) - 1) * matches, 1)
        slot_dest = owners * CAP + slot_rank
        sent_rows = (
            jnp.zeros((owner_count * CAP, row_width), jnp.float32).at[slot_dest].set(row_block)
        )
        sent_ids = (
            jnp.full((owner_count * CAP,), -1.0, jnp.float32)
            .at[slot_dest]
            .set(tiles.astype(jnp.float32))
        )
        return (sent_rows.reshape(owner_count, CAP, row_width), sent_ids.reshape(owner_count, CAP))

    sent_rows, sent_ids = jax.vmap(bucket)(
        laser_spot_holder[:, :, 0], laser_spot_patch, laser_energy_deposits
    )
    got_rows, got_ids = (
        lax.all_to_all(sent_rows, ("bx", "by"), split_axis=1, concat_axis=1, tiled=True),
        lax.all_to_all(sent_ids, ("bx", "by"), split_axis=1, concat_axis=1, tiled=True),
    )
    got_rows = got_rows.reshape(step_count, -1, row_width)
    got_ids = got_ids.reshape(step_count, -1)
    tile_iota = jnp.arange(patch_number, dtype=jnp.float32)
    equation_misfit = jnp.zeros_like(initial_thermal_state)
    matches = (got_ids[0][None, :] == tile_iota[:, None]).astype(jnp.float32)
    tile_heat = jnp.dot(
        matches, got_rows[0], precision=lax.Precision.HIGHEST, preferred_element_type=jnp.float32
    )
    energy_input = jnp.transpose(tile_heat.reshape(patch_number, 4, 64), (2, 0, 1)).reshape(
        64, patch_number * 4
    )
    diffuse_warmth = baseline_diffusivity * (1.0 + 0.5 * jnp.tanh(initial_thermal_state))
    interface_couplings = cond_links(diffuse_warmth, spacing)
    own_k = diffuse_warmth.reshape(-1)[voxel_lattice]
    home_thermal_state = initial_thermal_state.reshape(-1)[voxel_lattice]
    peer_k = lax.all_to_all(own_k, ("bx", "by"), split_axis=0, concat_axis=0, tiled=True)
    neighbor_thermal_state = lax.all_to_all(
        home_thermal_state, ("bx", "by"), split_axis=0, concat_axis=0, tiled=True
    )
    interface_diffusivity = areas * 0.5 * (own_k + peer_k)
    equation_misfit = energy_input - (
        inside_energy_current(initial_thermal_state, interface_couplings)
        + interface_energy_current(
            initial_thermal_state,
            voxel_lattice,
            interface_diffusivity,
            home_thermal_state,
            neighbor_thermal_state,
        )
    )
    conjugate_gradient_loop = initial_thermal_state

    def one_turn(turn_index, carry):
        conjugate_gradient_loop, equation_misfit, direction, res_norm = carry
        applied = apply_operator(
            direction, heat_mass, interface_couplings, voxel_lattice, interface_diffusivity
        )
        step_size = res_norm / lax.psum(jnp.sum(direction * applied), ("bx", "by"))
        conjugate_gradient_loop = conjugate_gradient_loop + step_size * direction
        equation_misfit = equation_misfit - step_size * applied
        next_norm = squares(equation_misfit)
        direction = equation_misfit + next_norm / res_norm * direction
        return (conjugate_gradient_loop, equation_misfit, direction, next_norm)

    start_norm = squares(equation_misfit)
    carry = one_turn(0, (conjugate_gradient_loop, equation_misfit, equation_misfit, start_norm))
    conjugate_gradient_loop, equation_misfit, direction, start_norm = lax.fori_loop(1, ITERS, one_turn, carry)
    return (conjugate_gradient_loop, equation_misfit)


def lanes_of(x, idx):
    return jnp.take_along_axis(x, idx, axis=1, mode="promise_in_bounds")


def thirds(x):
    a = x.astype(BF16)
    rest = x - a.astype(F32)
    b = rest.astype(BF16)
    c = (rest - b.astype(F32)).astype(BF16)
    return a, b, c


def iota(shape, dim):
    return lax.broadcasted_iota(I32, shape, dim)


def dot_nt(a, b):
    return lax.dot_general(a, b, (((1,), (1,)), ((), ())), preferred_element_type=F32)


def dot_nn(a, b):
    return jnp.dot(a, b, preferred_element_type=F32)


def peers():
    bx, by = lax.axis_index("bx"), lax.axis_index("by")
    offs = []
    for dc in range(2):
        for dy in range(4):
            for dx in range(4):
                for dz in range(4):
                    if (dc, dy, dx, dz) != (0, 0, 0, 0):
                        hops = min(dy, 4 - dy) + min(dx, 4 - dx) + min(dz, 4 - dz)
                        offs.append((-hops, dc, dy, dx, dz))
    offs.sort()
    y, core, x, z = bx // 2, lax.rem(bx, 2), by // 4, lax.rem(by, 4)
    for _, dc, dy, dx, dz in offs:
        px = lax.rem(y + dy, 4) * 2 + lax.rem(core + dc, 2)
        py = lax.rem(x + dx, 4) * 4 + lax.rem(z + dz, 4)
        yield px, py


def step_kernel(
    temp_hbm, base_hbm, store_hbm, level_hbm, face_hbm, area_hbm, rows_hbm, owner_hbm, tile_hbm,
    x_out, r_out, p_out, w_out, s_out, flag_out, scale_out,
    in_t, in_b, in_s, level, face, area, rows, owner, tile,
    xf, kf, mf, gx, gy, gz, ra, rb, wf, sf, pf, nat, en,
    ohs, ohl, celltab, lanetab, srcrow, srclane, rowid, slane, slots, slots2, msgs,
    ro, wo, wp, zo, gface, heat, oht, uf, zf, kept, keys, members,
    snd, rcv, lsnd, lrcv,
    in_sem, ssem, rsem, lssem, lrsem, out_sem,
):
    bx, by = lax.axis_index("bx"), lax.axis_index("by")
    me = bx * 16 + by
    barrier = pltpu.get_barrier_semaphore()
    def laser():
        return pltpu.make_async_remote_copy(
            src_ref=lsnd.at[pl.ds(0, 127)], dst_ref=lrcv.at[pl.ds(0, 127)],
            send_sem=lssem, recv_sem=lrsem, device_id=(lax.rem(bx + 1, 8), by), device_id_type=MESH,
        )

    def all_of(r):
        return pltpu.make_async_remote_copy(
            src_ref=snd.at[r, pl.ds(0, 127)], dst_ref=rcv.at[r, pl.ds(0, 127)],
            send_sem=ssem.at[r], recv_sem=rsem.at[r],
            device_id=(lax.rem(bx + 1, 8), by), device_id_type=MESH,
        )
    for px, py in peers():
        pl.semaphore_signal(barrier, inc=1, device_id=(px, py), device_id_type=MESH)

    loads = [
        pltpu.make_async_copy(src, dst, in_sem.at[i])
        for i, (src, dst) in enumerate(
            [(owner_hbm, owner), (tile_hbm, tile), (rows_hbm, rows), (face_hbm, face), (area_hbm, area), (level_hbm, level),
             (temp_hbm, in_t), (base_hbm, in_b), (store_hbm, in_s)]
        )
    ]
    for c in loads:
        c.start()

    for c in loads[:3]:
        c.wait()
    own = owner[...]
    match = iota((128, 256), 0) == own
    upto = (iota((256, 256), 0) <= iota((256, 256), 1)).astype(F32).astype(BF16)
    before = dot_nn(match.astype(F32).astype(BF16), upto) - 1.0
    rank = jnp.sum(jnp.where(match, before, 0.0), axis=0, keepdims=True)
    dest = own * CAP + rank.astype(I32)
    place = (iota((1024, 256), 0) == dest).astype(F32).astype(BF16)
    pieces = thirds(rows[...])
    put = (dot_nn(place, pieces[0]) + dot_nn(place, pieces[1])) + dot_nn(place, pieces[2])
    lsnd[...] = put.reshape(128, 8, 256)
    num = tile[...] + 1
    is_rank = iota((8, 256), 0) == rank.astype(I32)
    high = jnp.where(is_rank, num >> 5, 0).astype(F32)
    low = jnp.where(is_rank, num & 31, 0).astype(F32)
    hl = jnp.concatenate([high, low], axis=0).astype(BF16)
    ids = dot_nt(hl, match.astype(F32).astype(BF16))
    ids = ids[0:8] * 32.0 + ids[8:16] - 1.0

    for c in loads[3:6]:
        c.wait()
    fc = face[...]
    bt = (fc & 4095) >> 7
    for i in range(32):
        ohs[pl.ds(32 * i, 32), :] = (iota((32, 128), 0) == bt[i : i + 1]).astype(F32).astype(BF16)
    tri = (iota((128, 128), 0) <= iota((128, 128), 1)).astype(F32).astype(BF16)
    ones = jnp.ones((128, 128), BF16)
    run = jnp.zeros((32, 128), F32)
    ranks = []
    for i in range(32):
        oh = ohs[pl.ds(32 * i, 32), :]
        pre = dot_nn(oh, tri)
        ranks.append(jnp.sum(oh.astype(F32) * (pre + run - 1.0), axis=0, keepdims=True))
        run = run + dot_nn(oh, ones)
    rank = jnp.concatenate(ranks, axis=0).astype(I32)
    over = jnp.max(jnp.max((rank >= 256).astype(F32), axis=0, keepdims=True), axis=1, keepdims=True)
    rid = (rank >> 7) * 32 + bt
    rowid[...] = rid
    slane[...] = rank & 127
    cellv = (fc >> 12).astype(F32)
    lanev = (fc & 127).astype(F32)
    lane_f = iota((1, 128), 1).astype(F32)
    acc = jnp.zeros((256, 128), F32)
    for i in range(32):
        hit = iota((64, 128), 0) == rid[i : i + 1]
        a = jnp.concatenate(
            [
                jnp.where(hit, F32(i + 1), 0.0),
                jnp.where(hit, lane_f, 0.0),
                jnp.where(hit, cellv[i : i + 1], 0.0),
                jnp.where(hit, lanev[i : i + 1], 0.0),
            ],
            axis=0,
        ).astype(BF16)
        b = (iota((128, 128), 0) == slane[i : i + 1, :]).astype(F32).astype(BF16)
        acc = acc + dot_nt(a, b)
    tab = acc.astype(I32)
    filled = tab[0:64] > 0
    srcrow[...] = tab[0:64] - 1
    srclane[...] = tab[64:128]
    celltab[...] = jnp.where(filled, tab[128:192], -1)
    lanetab[...] = tab[192:256]

    def lane_hot(b, c):
        for h in range(2):
            row = lanetab[pl.ds(b + 32 * h, 1), :]
            ohl[pl.ds(b, 1), :, pl.ds(128 * h, 128)] = (
                (iota((128, 128), 0) == row).astype(F32).astype(BF16).reshape(1, 128, 128)
            )
        return c

    lax.fori_loop(0, 32, lane_hot, 0)

    for c in loads[6:]:
        c.wait()

    def prepare(k, c):
        lv = level[pl.ds(8 * k, 8), :]
        spacing = jnp.where(lv == 0, 1.0, jnp.where(lv == 1, 0.5, 0.25)).astype(F32)
        cube = spacing * spacing * spacing
        half = spacing * 0.5
        at = pl.ds(8 * k, 8)
        kv = {}
        for c in range(64):
            i, j, l = c // 16, (c // 4) % 4, c % 4
            where = pl.ds((c // 8) * 256 + c % 8 + 64 * k, 8, stride=8)
            t = in_t[where, :]
            kc = in_b[where, :] * (1.0 + 0.5 * jnp.tanh(t))
            xf[c, at, :] = t
            kf[c, at, :] = kc
            mf[c, at, :] = in_s[where, :] * cube
            kv[c] = kc
            if i:
                gx[c - 16, at, :] = half * (kc + kv.pop(c - 16))
            if j:
                gy[(i * 3 + j - 1) * 4 + l, at, :] = half * (kc + kv[c - 4])
            if l:
                gz[(i * 4 + j) * 3 + l - 1, at, :] = half * (kc + kv[c - 1])
        return 0

    lax.fori_loop(0, 4, prepare, 0)

    def gather(field, out):
        def group(k, c):
            at, at2 = pl.ds(8 * k, 8), pl.ds(32 + 8 * k, 8)
            l0, l1, c0, c1 = lanetab[at, :], lanetab[at2, :], celltab[at, :], celltab[at2, :]
            a0 = jnp.zeros((8, 128), F32)
            a1 = jnp.zeros((8, 128), F32)
            for cell in range(64):
                v = field[cell, at, :]
                a0 = jnp.where(c0 == cell, lanes_of(v, l0), a0)
                a1 = jnp.where(c1 == cell, lanes_of(v, l1), a1)
            out[at, :] = a0
            out[at2, :] = a1
            return c

        lax.fori_loop(0, 4, group, 0)

    def to_entries(src):
        outs = []
        for g in range(4):
            ri, la = rowid[8 * g : 8 * g + 8, :], slane[8 * g : 8 * g + 8, :]
            a = jnp.zeros((8, 128), F32)
            for t in range(64):
                row = jnp.broadcast_to(src[t : t + 1, :], (8, 128))
                a = jnp.where(ri == t, lanes_of(row, la), a)
            outs.append(a)
        return jnp.concatenate(outs, axis=0)

    def to_slots(src, out):
        for g in range(8):
            ri, la = srcrow[8 * g : 8 * g + 8, :], srclane[8 * g : 8 * g + 8, :]
            a = jnp.zeros((8, 128), F32)
            for t in range(32):
                row = jnp.broadcast_to(src[t : t + 1, :], (8, 128))
                a = jnp.where(ri == t, lanes_of(row, la), a)
            out[8 * g : 8 * g + 8, :] = a

    def scatter(flux):
        def one(b, c):
            parts = [[], [], []]
            for h in range(2):
                row = flux[pl.ds(b + 32 * h, 1), :]
                hit = iota((64, 128), 0) == celltab[pl.ds(b + 32 * h, 1), :]
                p0 = row.astype(BF16).astype(F32)
                p1 = (row - p0).astype(BF16).astype(F32)
                p2 = row - p0 - p1
                for q, p in enumerate((p0, p1, p2)):
                    parts[q].append(jnp.where(hit, p, 0.0))
            a = jnp.concatenate([jnp.concatenate(p, axis=1) for p in parts], axis=0).astype(BF16)
            o = dot_nt(a, ohl[b])
            nat[pl.ds(64 * b, 64), :] = (o[0:64] + o[64:128]) + o[128:192]
            return c

        lax.fori_loop(0, 32, one, 0, unroll=4)

    def stencil(k, load, emit, mass):
        at = pl.ds(8 * k, 8)
        v, acc = {}, {}
        for c in range(64):
            i, j, l = c // 16, (c // 4) % 4, c % 4
            v[c] = load(c)
            a = mf[c, at, :] * v[c] if mass else jnp.zeros((8, 128), F32)
            if l:
                f = gz[(i * 4 + j) * 3 + l - 1, at, :] * (v[c] - v[c - 1])
                a, acc[c - 1] = a + f, acc[c - 1] - f
            if j:
                f = gy[(i * 3 + j - 1) * 4 + l, at, :] * (v[c] - v[c - 4])
                a, acc[c - 4] = a + f, acc[c - 4] - f
            if i:
                f = gx[c - 16, at, :] * (v[c] - v.pop(c - 16))
                a = a + f
                emit(c - 16, acc.pop(c - 16) - f)
            acc[c] = a
        for c in range(48, 64):
            emit(c, acc[c])

    def send(r, feats):
        n = sum(f.shape[0] for f in feats)
        full = jnp.concatenate(list(feats) + [jnp.zeros((128 - n, 128), F32)], axis=0)
        snd[r] = full.T
        rcv[r, pl.ds(me, 1), :] = snd[r, pl.ds(me, 1), :]
        for px, py in peers():
            pltpu.make_async_remote_copy(
                src_ref=snd.at[r, pl.ds(px * 16 + py, 1)], dst_ref=rcv.at[r, pl.ds(me, 1)],
                send_sem=ssem.at[r], recv_sem=rsem.at[r], device_id=(px, py), device_id_type=MESH,
            ).start()

    def receive(r):
        all_of(r).wait_recv()
        return rcv[r].T

    def total(rows):
        return jnp.sum(rows, axis=1, keepdims=True)

    def same_cell():
        key = jnp.where(celltab[...] >= 0, celltab[...] * 128 + lanetab[...], -1)
        keyt = key.astype(F32).T
        most = jnp.zeros((1, 128), I32)
        big = 1 << 20
        kept[...] = keyt
        keys[...] = key.astype(F32)

        def one(b, most):
            cols = []
            for h in range(2):
                hit = (iota((128, 64), 1) == b + 32 * h)
                cols.append(jnp.sum(jnp.where(hit, kept[...], 0.0), axis=1, keepdims=True))
            for h in range(2):
                row = keys[pl.ds(b + 32 * h, 1), :]
                cands = []
                for g in range(2):
                    same = jnp.logical_and(cols[g] == row, row >= 0.0)
                    cands.append(jnp.where(same, iota((128, 128), 0) + 128 * g, big))
                cand = jnp.concatenate(cands, axis=0)
                for d in range(MEMBERS):
                    low = jnp.min(cand, axis=0, keepdims=True)
                    members[d, pl.ds(b + 32 * h, 1), :] = low
                    cand = jnp.where(cand > low, cand, big)
                most = jnp.maximum(most, (jnp.min(cand, axis=0, keepdims=True) < big).astype(I32))
            return most

        most = lax.fori_loop(0, 32, one, most)
        return jnp.max(most.astype(F32), axis=1, keepdims=True)

    def joined(f):
        tops, lows = [], []
        for g in range(4):
            halves = [f[8 * g : 8 * g + 8, :], f[32 + 8 * g : 40 + 8 * g, :]]
            for h, outs in ((0, tops), (1, lows)):
                a = jnp.zeros((8, 128), F32)
                for d in range(MEMBERS):
                    m = members[d, pl.ds(32 * h + 8 * g, 8), :]
                    at = m & 127
                    v = jnp.where(m < 128, lanes_of(halves[0], at), lanes_of(halves[1], at))
                    a = a + jnp.where(m < 256, v, 0.0)
                outs.append(a)
        return jnp.concatenate(tops + lows, axis=0)

    def dot_all(v):
        return jnp.sum(jnp.sum(v, axis=0, keepdims=True), axis=1, keepdims=True)

    def spread(v):
        return jnp.broadcast_to(v, (8, 128))

    zero = jnp.zeros((8, 128), F32)
    gather(kf, slots)
    gather(xf, slots2)
    round0 = [to_entries(slots), to_entries(slots2), ids]
    pl.semaphore_wait(barrier, 127)
    lrcv[pl.ds(me, 1)] = lsnd[pl.ds(me, 1)]
    for n, (px, py) in enumerate(peers()):
        if n == 48:
            send(0, round0)
        pltpu.make_async_remote_copy(
            src_ref=lsnd.at[pl.ds(px * 16 + py, 1)], dst_ref=lrcv.at[pl.ds(me, 1)],
            send_sem=lssem, recv_sem=lrsem, device_id=(px, py), device_id_type=MESH,
        ).start()
    many = same_cell()
    msgs[...] = receive(0)
    to_slots(msgs.at[pl.ds(0, 32)], gface)
    to_slots(msgs.at[pl.ds(32, 32)], wp)
    to_slots(area, wo)
    gface[...] = wo[...] * 0.5 * (slots[...] + gface[...])
    slots[...] = gface[...] * (slots2[...] - wp[...])
    scatter(slots)
    tids = msgs[64:72, :].astype(I32)
    for j in range(8):
        oht[:, pl.ds(128 * j, 128)] = (iota((1024, 128), 0) == tids[j : j + 1]).astype(F32).astype(BF16)

    def first(k, c):
        at = pl.ds(8 * k, 8)

        def emit(c, a):
            rb[c, at, :] = a + nat[pl.ds(512 * k + c, 8, stride=64), :]

        stencil(k, lambda c: xf[c, at, :], emit, False)
        return c

    lax.fori_loop(0, 4, first, 0)
    laser().wait_recv()
    by_rank = []
    for j in range(8):
        by_rank.append(lrcv[:, j, :])
    pieces = thirds(jnp.concatenate(by_rank, axis=0))
    for q in range(8):
        o = oht[pl.ds(128 * q, 128), :]
        h = (dot_nn(o, pieces[0]) + dot_nn(o, pieces[1])) + dot_nn(o, pieces[2])
        for part in range(4):
            heat[pl.ds(512 * q + part, 128, stride=4), :] = h[:, 64 * part : 64 * part + 64]
        for b in range(4 * q, 4 * q + 4):
            en[64 * b : 64 * b + 64, :] = heat[128 * b : 128 * b + 128, :].T

    def start(k, c):
        at = pl.ds(8 * k, 8)
        for c in range(64):
            ra[c, at, :] = en[pl.ds(512 * k + c, 8, stride=64), :] - rb[c, at, :]
        return 0

    lax.fori_loop(0, 4, start, 0)
    gather(ra, ro)
    send(1, [to_entries(ro), spread(jnp.maximum(over, many))])

    def early(k, sums):
        at = pl.ds(8 * k, 8)
        s = list(sums)

        def emit(c, a):
            r = ra[c, at, :]
            wf[c, at, :] = a
            s[0] = s[0] + r * r
            s[1] = s[1] + r * a

        stencil(k, lambda c: ra[c, at, :], emit, True)
        return tuple(s)

    rr, rw = [dot_all(v) for v in lax.fori_loop(0, 4, early, (zero, zero))]
    gather(wf, wo)
    msgs[...] = receive(1)
    flag_out[...] = spread(jnp.max(msgs[32:40, :], axis=1, keepdims=True))
    to_slots(msgs.at[pl.ds(0, 32)], wp)
    flux = gface[...] * (ro[...] - wp[...])
    slots[...] = flux
    rw = rw + dot_all(ro[...] * flux)
    wo[...] = wo[...] + joined(flux)

    old_rr = old_alpha = alpha1 = beta1 = None
    r_now, r_next = ra, rb
    for it in range(ITERS):
        last = it == ITERS - 1
        if last:
            send(it + 2, [spread(rr), spread(rw)])
        else:
            send(it + 2, [to_entries(wo), spread(rr), spread(rw)])
        scatter(slots)
        if it:
            r_now, r_next = r_next, r_now
            alpha, beta = spread(alpha1), None if it == 1 else spread(beta1)

        def along(k, sums, it=it, last=last, r_now=r_now, r_next=r_next):
            at = pl.ds(8 * k, 8)
            d = list(sums)

            def load(c):
                here = nat[pl.ds(512 * k + c, 8, stride=64), :]
                if it == 0:
                    w = wf[c, at, :] + here
                    wf[c, at, :] = w
                    d[2] = d[2] + w * w
                    return w
                w = wf[c, at, :]
                z = uf[c, at, :] + here
                s = w
                r = r_next[c, at, :]
                q = r
                if it > 1:
                    z = z + beta * zf[c, at, :]
                    s = s + beta * sf[c, at, :]
                    q = q + beta * pf[c, at, :]
                pf[c, at, :] = q
                xf[c, at, :] = xf[c, at, :] + alpha * q
                sf[c, at, :] = s
                r = r - alpha * s
                w = w - alpha * z
                r_now[c, at, :] = r
                wf[c, at, :] = w
                if not last:
                    zf[c, at, :] = z
                    for n, (p, q) in enumerate(((r, r), (r, w), (w, w), (r, s), (w, s), (s, s), (w, z), (s, z))):
                        d[n] = d[n] + p * q
                return w

            def emit(c, a):
                uf[c, at, :] = a
                d[8] = d[8] + wf[c, at, :] * a

            if last:
                for c in range(64):
                    load(c)
            else:
                stencil(k, load, emit, True)
            return tuple(d)

        dots = lax.fori_loop(0, 4, along, (zero,) * 9)
        if last:
            outs = [
                pltpu.make_async_copy(src, dst, out_sem.at[n])
                for n, (src, dst) in enumerate(zip((xf, r_now, pf, wf, sf), (x_out, r_out, p_out, w_out, s_out)))
            ]
            for c in outs:
                c.start()
        else:
            dots = [dot_all(v) for v in dots]
            if it == 0:
                dots[0], dots[1] = rr, rw
            gather(uf, slots2)
        msgs[...] = receive(it + 2)
        base = 0 if last else 32
        g_rr, g_rw = total(msgs[base : base + 1, :]), total(msgs[base + 8 : base + 9, :])
        if it:
            beta1 = g_rr / old_rr
            alpha1 = g_rr / (g_rw - beta1 * g_rr / old_alpha)
        else:
            alpha1 = g_rr / g_rw
        old_rr, old_alpha = g_rr, alpha1
        if last:
            break
        to_slots(msgs.at[pl.ds(0, 32)], wp)
        flux = gface[...] * (wo[...] - wp[...])
        slots[...] = flux
        rr, rw, ww, rs, ws, ss, wz, sz, wu = dots
        wq = wu + dot_all(wo[...] * flux)
        z = slots2[...] + joined(flux)
        s = wo[...]
        if it:
            z = z + beta1 * zo[...]
            rs = rw + beta1 * rs
            ss = ww + beta1 * (2.0 * ws + beta1 * ss)
            sz = wq + beta1 * (2.0 * wz + beta1 * sz)
            ws = ww + beta1 * ws
        else:
            rs, ss, sz, ws = rw, ww, wq, ww
        zo[...] = z
        wo[...] = s - alpha1 * z
        rr = rr + alpha1 * (alpha1 * ss - 2.0 * rs)
        rw = rw + alpha1 * (alpha1 * sz - 2.0 * ws)

    scale_out[0:8, :] = spread(alpha1)
    scale_out[8:16, :] = spread(beta1)
    for r in range(ROUNDS):
        all_of(r).wait_send()
    laser().wait_send()
    for c in outs:
        c.wait()


def finish_kernel(scale, x, r, p, w, s, x_out, r_out):
    alpha, beta = scale[0:8, :], scale[8:16, :]
    for c in range(64):
        to = pl.ds(c % 8, 8, stride=8)
        x_out[c // 8, to, :] = x[c] + alpha * (r[c] + beta * p[c])
        r_out[c // 8, to, :] = r[c] - alpha * (w[c] + beta * s[c])


def finish(scale, *fields):
    of = pl.BlockSpec((64, 8, 128), lambda k: (0, k, 0))
    to = pl.BlockSpec((8, 64, 128), lambda k: (0, k, 0))
    x, r = pl.pallas_call(
        finish_kernel,
        grid=(4,),
        out_shape=[jax.ShapeDtypeStruct((8, 256, 128), F32)] * 2,
        in_specs=[pl.BlockSpec((16, 128), lambda k: (0, 0))] + [of] * 5,
        out_specs=[to] * 2,
    )(scale, *fields)
    return untiled(x), untiled(r)


def tiled(v):
    return v.reshape(8, 8, 32, 128).transpose(0, 2, 1, 3).reshape(2048, 128)


def untiled(v):
    return v.reshape(8, 32, 8, 128).transpose(0, 2, 1, 3).reshape(64, 4096)


def vm(*shape, dtype=F32):
    return pltpu.VMEM(shape, dtype)


def shards(*args):
    temp, base, store, level, face, area, rows, owner, tile = args
    field = lambda: vm(64, 32, 128)
    part = lambda: vm(48, 32, 128)
    slot = lambda dtype=F32: vm(64, 128, dtype=dtype)
    *fields, flag, scale = pl.pallas_call(
        step_kernel,
        out_shape=[
            *[jax.ShapeDtypeStruct((64, 32, 128), F32)] * 5,
            jax.ShapeDtypeStruct((8, 128), F32),
            jax.ShapeDtypeStruct((16, 128), F32),
        ],
        in_specs=[pl.BlockSpec(memory_space=pl.ANY)] * 9,
        out_specs=[pl.BlockSpec(memory_space=pl.ANY)] * 5 + [pl.BlockSpec(memory_space=pltpu.VMEM)] * 2,
        scratch_shapes=[
            vm(2048, 128), vm(2048, 128), vm(2048, 128),
            vm(32, 128, dtype=I32), vm(32, 128, dtype=I32), vm(32, 128), vm(256, 256),
            vm(1, 256, dtype=I32), vm(1, 256, dtype=I32),
            field(), field(), field(), part(), part(), part(),
            field(), field(), field(), field(), field(), vm(2048, 128), vm(2048, 128),
            vm(1024, 128, dtype=BF16), vm(32, 128, 256, dtype=BF16),
            slot(I32), slot(I32), slot(I32), slot(I32), vm(32, 128, dtype=I32), vm(32, 128, dtype=I32),
            slot(), slot(), vm(128, 128),
            slot(), slot(), slot(), slot(), slot(), vm(4096, 64), vm(1024, 1024, dtype=BF16),
            field(), field(), vm(128, 64), slot(), vm(MEMBERS, 64, 128, dtype=I32),
            vm(ROUNDS, 128, 128), vm(ROUNDS, 128, 128), vm(128, 8, 256), vm(128, 8, 256),
            pltpu.SemaphoreType.DMA((9,)),
            pltpu.SemaphoreType.DMA((ROUNDS,)),
            pltpu.SemaphoreType.DMA((ROUNDS,)),
            pltpu.SemaphoreType.DMA,
            pltpu.SemaphoreType.DMA,
            pltpu.SemaphoreType.DMA((5,)),
        ],
        compiler_params=pltpu.CompilerParams(
            collective_id=0, has_side_effects=True, vmem_limit_bytes=63 * 1024 * 1024
        ),
    )(
        tiled(temp), tiled(base), tiled(store), level.reshape(32, 128),
        face[0].T, area[0].T, rows[0], owner.reshape(1, 256), tile,
    )
    return lax.cond(
        flag[0, 0] > 0.5,
        lambda: general(*args),
        lambda: finish(scale, *fields),
    )


def solution(mesh):
    return jax.shard_map(
        shards,
        mesh=mesh,
        in_specs=(
            P(None, ("bx", "by")),
            P(None, ("bx", "by")),
            P(None, ("bx", "by")),
            P(("bx", "by")),
            P(("bx", "by"), None, None),
            P(("bx", "by"), None, None),
            P(None, ("bx", "by"), None),
            P(None, ("bx", "by"), None),
            P(None, ("bx", "by")),
        ),
        out_specs=(P(None, ("bx", "by")), P(None, ("bx", "by"))),
        check_vma=False,
    )
```

```python
import functools

import jax
import jax.numpy as jnp
from jax import lax
from jax.experimental import pallas as pl
from jax.experimental.pallas import tpu as pltpu
from jax.sharding import PartitionSpec as P

CAP = 8
ITERS = 4
MESH = pl.DeviceIdType.MESH
F32, BF16, I32 = jnp.float32, jnp.bfloat16, jnp.int32
ROUNDS = 6


def cond_links(diffuse_warmth, spacing):
    grid_cube = diffuse_warmth.reshape(4, 4, 4, -1)
    first_pairs = spacing * 0.5 * (grid_cube[1:] + grid_cube[:-1])
    second_pairs = spacing * 0.5 * (grid_cube[:, 1:] + grid_cube[:, :-1])
    third_pairs = spacing * 0.5 * (grid_cube[:, :, 1:] + grid_cube[:, :, :-1])
    return (first_pairs, second_pairs, third_pairs)


def inside_energy_current(values, interface_couplings):
    grid_cube = values.reshape(4, 4, 4, -1)
    flux_one = interface_couplings[0] * (grid_cube[1:] - grid_cube[:-1])
    flux_two = interface_couplings[1] * (grid_cube[:, 1:] - grid_cube[:, :-1])
    flux_three = interface_couplings[2] * (grid_cube[:, :, 1:] - grid_cube[:, :, :-1])
    zero_pad = (0, 0)
    balance = jnp.pad(flux_one, ((1, 0), zero_pad, zero_pad, zero_pad)) - jnp.pad(
        flux_one, ((0, 1), zero_pad, zero_pad, zero_pad)
    )
    balance = (
        balance
        + jnp.pad(flux_two, (zero_pad, (1, 0), zero_pad, zero_pad))
        - jnp.pad(flux_two, (zero_pad, (0, 1), zero_pad, zero_pad))
    )
    balance = (
        balance
        + jnp.pad(flux_three, (zero_pad, zero_pad, (1, 0), zero_pad))
        - jnp.pad(flux_three, (zero_pad, zero_pad, (0, 1), zero_pad))
    )
    return balance.reshape(values.shape)


def interface_energy_current(values, voxel_lattice, interface_diffusivity, own_vals, peer_vals):
    flux_vals = interface_diffusivity * (own_vals - peer_vals)
    flat_zero = jnp.zeros((values.size,), jnp.float32)
    return flat_zero.at[voxel_lattice.reshape(-1)].add(flux_vals.reshape(-1)).reshape(values.shape)


def apply_operator(values, heat_mass, interface_couplings, voxel_lattice, interface_diffusivity):
    own_vals = values.reshape(-1)[voxel_lattice]
    peer_vals = lax.all_to_all(own_vals, ("bx", "by"), split_axis=0, concat_axis=0, tiled=True)
    return (
        heat_mass * values
        + inside_energy_current(values, interface_couplings)
        + interface_energy_current(
            values, voxel_lattice, interface_diffusivity, own_vals, peer_vals
        )
    )


def squares(values):
    return lax.psum(jnp.sum(values * values), ("bx", "by"))


def general(
    initial_thermal_state,
    baseline_diffusivity,
    thermal_storage,
    refinement_depth,
    interface_voxel_table,
    interface_weighting,
    laser_energy_deposits,
    laser_spot_holder,
    laser_spot_patch,
):
    owner_count = lax.axis_size(("bx", "by"))
    voxel_lattice = interface_voxel_table[0]
    areas = interface_weighting[0]
    patch_number = initial_thermal_state.shape[1] // 4
    step_count = laser_energy_deposits.shape[0]
    row_width = laser_energy_deposits.shape[2]
    spacing = 0.5 ** refinement_depth.astype(jnp.float32)
    heat_mass = thermal_storage * spacing**3

    def bucket(owners, tiles, row_block):
        matches = (owners[:, None] == jnp.arange(owner_count, dtype=jnp.int32)[None, :]).astype(
            jnp.int32
        )
        slot_rank = jnp.sum((jnp.cumsum(matches, 0) - 1) * matches, 1)
        slot_dest = owners * CAP + slot_rank
        sent_rows = (
            jnp.zeros((owner_count * CAP, row_width), jnp.float32).at[slot_dest].set(row_block)
        )
        sent_ids = (
            jnp.full((owner_count * CAP,), -1.0, jnp.float32)
            .at[slot_dest]
            .set(tiles.astype(jnp.float32))
        )
        return (sent_rows.reshape(owner_count, CAP, row_width), sent_ids.reshape(owner_count, CAP))

    sent_rows, sent_ids = jax.vmap(bucket)(
        laser_spot_holder[:, :, 0], laser_spot_patch, laser_energy_deposits
    )
    got_rows, got_ids = (
        lax.all_to_all(sent_rows, ("bx", "by"), split_axis=1, concat_axis=1, tiled=True),
        lax.all_to_all(sent_ids, ("bx", "by"), split_axis=1, concat_axis=1, tiled=True),
    )
    got_rows = got_rows.reshape(step_count, -1, row_width)
    got_ids = got_ids.reshape(step_count, -1)
    tile_iota = jnp.arange(patch_number, dtype=jnp.float32)
    equation_misfit = jnp.zeros_like(initial_thermal_state)
    matches = (got_ids[0][None, :] == tile_iota[:, None]).astype(jnp.float32)
    tile_heat = jnp.dot(
        matches, got_rows[0], precision=lax.Precision.HIGHEST, preferred_element_type=jnp.float32
    )
    energy_input = jnp.transpose(tile_heat.reshape(patch_number, 4, 64), (2, 0, 1)).reshape(
        64, patch_number * 4
    )
    diffuse_warmth = baseline_diffusivity * (1.0 + 0.5 * jnp.tanh(initial_thermal_state))
    interface_couplings = cond_links(diffuse_warmth, spacing)
    own_k = diffuse_warmth.reshape(-1)[voxel_lattice]
    home_thermal_state = initial_thermal_state.reshape(-1)[voxel_lattice]
    peer_k = lax.all_to_all(own_k, ("bx", "by"), split_axis=0, concat_axis=0, tiled=True)
    neighbor_thermal_state = lax.all_to_all(
        home_thermal_state, ("bx", "by"), split_axis=0, concat_axis=0, tiled=True
    )
    interface_diffusivity = areas * 0.5 * (own_k + peer_k)
    equation_misfit = energy_input - (
        inside_energy_current(initial_thermal_state, interface_couplings)
        + interface_energy_current(
            initial_thermal_state,
            voxel_lattice,
            interface_diffusivity,
            home_thermal_state,
            neighbor_thermal_state,
        )
    )
    conjugate_gradient_loop = initial_thermal_state

    def one_turn(turn_index, carry):
        conjugate_gradient_loop, equation_misfit, direction, res_norm = carry
        applied = apply_operator(
            direction, heat_mass, interface_couplings, voxel_lattice, interface_diffusivity
        )
        step_size = res_norm / lax.psum(jnp.sum(direction * applied), ("bx", "by"))
        conjugate_gradient_loop = conjugate_gradient_loop + step_size * direction
        equation_misfit = equation_misfit - step_size * applied
        next_norm = squares(equation_misfit)
        direction = equation_misfit + next_norm / res_norm * direction
        return (conjugate_gradient_loop, equation_misfit, direction, next_norm)

    start_norm = squares(equation_misfit)
    carry = one_turn(0, (conjugate_gradient_loop, equation_misfit, equation_misfit, start_norm))
    conjugate_gradient_loop, equation_misfit, direction, start_norm = lax.fori_loop(1, ITERS, one_turn, carry)
    return (conjugate_gradient_loop, equation_misfit)


def lanes_of(x, idx):
    return jnp.take_along_axis(x, idx, axis=1, mode="promise_in_bounds")


def thirds(x):
    a = x.astype(BF16)
    rest = x - a.astype(F32)
    b = rest.astype(BF16)
    c = (rest - b.astype(F32)).astype(BF16)
    return a, b, c


def iota(shape, dim):
    return lax.broadcasted_iota(I32, shape, dim)


def dot_nt(a, b):
    return lax.dot_general(a, b, (((1,), (1,)), ((), ())), preferred_element_type=F32)


def dot_nn(a, b):
    return jnp.dot(a, b, preferred_element_type=F32)


def peers():
    bx, by = lax.axis_index("bx"), lax.axis_index("by")
    offs = []
    for dc in range(2):
        for dy in range(4):
            for dx in range(4):
                for dz in range(4):
                    if (dc, dy, dx, dz) != (0, 0, 0, 0):
                        hops = min(dy, 4 - dy) + min(dx, 4 - dx) + min(dz, 4 - dz)
                        offs.append((-hops, dc, dy, dx, dz))
    offs.sort()
    y, core, x, z = bx // 2, lax.rem(bx, 2), by // 4, lax.rem(by, 4)
    ys = [lax.rem(y + d, 4) * 2 for d in range(4)]
    cores = [lax.rem(core + d, 2) for d in range(2)]
    xs = [lax.rem(x + d, 4) * 4 for d in range(4)]
    zs = [lax.rem(z + d, 4) for d in range(4)]
    pxs = [[ys[d] + cores[e] for e in range(2)] for d in range(4)]
    pys = [[xs[d] + zs[e] for e in range(4)] for d in range(4)]
    return [(pxs[dy][dc], pys[dx][dz], pxs[dy][dc] * 16 + pys[dx][dz]) for _, dc, dy, dx, dz in offs]


def step_kernel(
    temp_hbm, base_hbm, store_hbm, level_hbm, face_hbm, area_hbm, rows_hbm, owner_hbm, tile_hbm,
    x_out, r_out, p_out, w_out, s_out, flag_out, scale_out,
    in_t, in_b, in_s, level, face, area, rows, owner, tile,
    xf, kf, mf, gx, gy, gz, ra, rb, wf, sf, pf, nat, en,
    ohs, ohl, celltab, lanetab, srcrow, srclane, rowid, slane, slots, slots2, msgs,
    ro, wo, zo, gface, flows, heat, oht, uf, zf, kept, keys, place_of, list_row, list_lane, mates,
    snd, rcv, lsnd, lrcv,
    in_sem, ssem, rsem, lssem, lrsem, out_sem,
):
    bx, by = lax.axis_index("bx"), lax.axis_index("by")
    me = bx * 16 + by
    barrier = pltpu.get_barrier_semaphore()
    def laser():
        return pltpu.make_async_remote_copy(
            src_ref=lsnd.at[pl.ds(0, 127)], dst_ref=lrcv.at[pl.ds(0, 127)],
            send_sem=lssem, recv_sem=lrsem, device_id=(lax.rem(bx + 1, 8), by), device_id_type=MESH,
        )

    def all_of(r):
        return pltpu.make_async_remote_copy(
            src_ref=snd.at[r, pl.ds(0, 127)], dst_ref=rcv.at[r, pl.ds(0, 127)],
            send_sem=ssem.at[r], recv_sem=rsem.at[r],
            device_id=(lax.rem(bx + 1, 8), by), device_id_type=MESH,
        )
    others = peers()
    for px, py, _ in others:
        pl.semaphore_signal(barrier, inc=1, device_id=(px, py), device_id_type=MESH)

    loads = [
        pltpu.make_async_copy(src, dst, in_sem.at[i])
        for i, (src, dst) in enumerate(
            [(owner_hbm, owner), (tile_hbm, tile), (rows_hbm, rows), (face_hbm, face), (area_hbm, area), (level_hbm, level),
             (temp_hbm, in_t), (base_hbm, in_b), (store_hbm, in_s)]
        )
    ]
    for c in loads:
        c.start()

    for c in loads[:3]:
        c.wait()
    own = owner[...]
    match = iota((128, 256), 0) == own
    upto = (iota((256, 256), 0) <= iota((256, 256), 1)).astype(F32).astype(BF16)
    before = dot_nn(match.astype(F32).astype(BF16), upto) - 1.0
    rank = jnp.sum(jnp.where(match, before, 0.0), axis=0, keepdims=True)
    dest = own * CAP + rank.astype(I32)
    place = (iota((1024, 256), 0) == dest).astype(F32).astype(BF16)
    pieces = thirds(rows[...])
    put = (dot_nn(place, pieces[0]) + dot_nn(place, pieces[1])) + dot_nn(place, pieces[2])
    lsnd[...] = put.reshape(128, 8, 256)
    num = tile[...] + 1
    is_rank = iota((8, 256), 0) == rank.astype(I32)
    high = jnp.where(is_rank, num >> 5, 0).astype(F32)
    low = jnp.where(is_rank, num & 31, 0).astype(F32)
    hl = jnp.concatenate([high, low], axis=0).astype(BF16)
    ids = dot_nt(hl, match.astype(F32).astype(BF16))
    ids = ids[0:8] * 32.0 + ids[8:16] - 1.0

    for c in loads[3:6]:
        c.wait()
    fc = face[...]
    bt = (fc & 4095) >> 7
    for i in range(32):
        ohs[pl.ds(32 * i, 32), :] = (iota((32, 128), 0) == bt[i : i + 1]).astype(F32).astype(BF16)
    tri = (iota((128, 128), 0) <= iota((128, 128), 1)).astype(F32).astype(BF16)
    ones = jnp.ones((128, 128), BF16)
    run = jnp.zeros((32, 128), F32)
    ranks = []
    for i in range(32):
        oh = ohs[pl.ds(32 * i, 32), :]
        pre = dot_nn(oh, tri)
        ranks.append(jnp.sum(oh.astype(F32) * (pre + run - 1.0), axis=0, keepdims=True))
        run = run + dot_nn(oh, ones)
    rank = jnp.concatenate(ranks, axis=0).astype(I32)
    over = jnp.max(jnp.max((rank >= 256).astype(F32), axis=0, keepdims=True), axis=1, keepdims=True)
    rid = (rank >> 7) * 32 + bt
    rowid[...] = rid
    slane[...] = rank & 127
    cellv = (fc >> 12).astype(F32)
    lanev = (fc & 127).astype(F32)
    lane_f = iota((1, 128), 1).astype(F32)
    acc = jnp.zeros((256, 128), F32)
    for i in range(32):
        hit = iota((64, 128), 0) == rid[i : i + 1]
        a = jnp.concatenate(
            [
                jnp.where(hit, F32(i + 1), 0.0),
                jnp.where(hit, lane_f, 0.0),
                jnp.where(hit, cellv[i : i + 1], 0.0),
                jnp.where(hit, lanev[i : i + 1], 0.0),
            ],
            axis=0,
        ).astype(BF16)
        b = (iota((128, 128), 0) == slane[i : i + 1, :]).astype(F32).astype(BF16)
        acc = acc + dot_nt(a, b)
    tab = acc.astype(I32)
    filled = tab[0:64] > 0
    srcrow[...] = tab[0:64] - 1
    srclane[...] = tab[64:128]
    celltab[...] = jnp.where(filled, tab[128:192], -1)
    lanetab[...] = tab[192:256]

    def lane_hot(b, c):
        for h in range(2):
            row = lanetab[pl.ds(b + 32 * h, 1), :]
            ohl[pl.ds(b, 1), :, pl.ds(128 * h, 128)] = (
                (iota((128, 128), 0) == row).astype(F32).astype(BF16).reshape(1, 128, 128)
            )
        return c

    lax.fori_loop(0, 32, lane_hot, 0)

    for c in loads[6:]:
        c.wait()

    def prepare(k, c):
        lv = level[pl.ds(8 * k, 8), :]
        spacing = jnp.where(lv == 0, 1.0, jnp.where(lv == 1, 0.5, 0.25)).astype(F32)
        cube = spacing * spacing * spacing
        half = spacing * 0.5
        at = pl.ds(8 * k, 8)
        kv = {}
        for c in range(64):
            i, j, l = c // 16, (c // 4) % 4, c % 4
            where = pl.ds((c // 8) * 256 + c % 8 + 64 * k, 8, stride=8)
            t = in_t[where, :]
            kc = in_b[where, :] * (1.0 + 0.5 * jnp.tanh(t))
            xf[c, at, :] = t
            kf[c, at, :] = kc
            mf[c, at, :] = in_s[where, :] * cube
            kv[c] = kc
            if i:
                gx[c - 16, at, :] = half * (kc + kv.pop(c - 16))
            if j:
                gy[(i * 3 + j - 1) * 4 + l, at, :] = half * (kc + kv[c - 4])
            if l:
                gz[(i * 4 + j) * 3 + l - 1, at, :] = half * (kc + kv[c - 1])
        return 0

    lax.fori_loop(0, 4, prepare, 0)

    def gather(field, out):
        def group(k, c):
            at, at2 = pl.ds(8 * k, 8), pl.ds(32 + 8 * k, 8)
            l0, l1, c0, c1 = lanetab[at, :], lanetab[at2, :], celltab[at, :], celltab[at2, :]
            a0 = jnp.zeros((8, 128), F32)
            a1 = jnp.zeros((8, 128), F32)
            for cell in range(64):
                v = field[cell, at, :]
                a0 = jnp.where(c0 == cell, lanes_of(v, l0), a0)
                a1 = jnp.where(c1 == cell, lanes_of(v, l1), a1)
            out[at, :] = a0
            out[at2, :] = a1
            return c

        lax.fori_loop(0, 4, group, 0)

    def to_entries(src):
        outs = []
        for g in range(4):
            ri, la = rowid[8 * g : 8 * g + 8, :], slane[8 * g : 8 * g + 8, :]
            a = jnp.zeros((8, 128), F32)
            for t in range(64):
                row = jnp.broadcast_to(src[t : t + 1, :], (8, 128))
                a = jnp.where(ri == t, lanes_of(row, la), a)
            outs.append(a)
        return jnp.concatenate(outs, axis=0)

    def to_slots(src, out):
        for g in range(8):
            ri, la = srcrow[8 * g : 8 * g + 8, :], srclane[8 * g : 8 * g + 8, :]
            a = jnp.zeros((8, 128), F32)
            for t in range(32):
                row = jnp.broadcast_to(src[t : t + 1, :], (8, 128))
                a = jnp.where(ri == t, lanes_of(row, la), a)
            out[8 * g : 8 * g + 8, :] = a

    def scatter(flux):
        def one(b, c):
            parts = [[], [], []]
            for h in range(2):
                row = flux[pl.ds(b + 32 * h, 1), :]
                hit = iota((64, 128), 0) == celltab[pl.ds(b + 32 * h, 1), :]
                p0 = row.astype(BF16).astype(F32)
                p1 = (row - p0).astype(BF16).astype(F32)
                p2 = row - p0 - p1
                for q, p in enumerate((p0, p1, p2)):
                    parts[q].append(jnp.where(hit, p, 0.0))
            a = jnp.concatenate([jnp.concatenate(p, axis=1) for p in parts], axis=0).astype(BF16)
            o = dot_nt(a, ohl[b])
            nat[pl.ds(64 * b, 64), :] = (o[0:64] + o[64:128]) + o[128:192]
            return c

        lax.fori_loop(0, 32, one, 0, unroll=16)

    def stencil(k, load, emit, mass):
        at = pl.ds(8 * k, 8)
        v, acc = {}, {}
        for c in range(64):
            i, j, l = c // 16, (c // 4) % 4, c % 4
            v[c] = load(c)
            a = mf[c, at, :] * v[c] if mass else jnp.zeros((8, 128), F32)
            if l:
                f = gz[(i * 4 + j) * 3 + l - 1, at, :] * (v[c] - v[c - 1])
                a, acc[c - 1] = a + f, acc[c - 1] - f
            if j:
                f = gy[(i * 3 + j - 1) * 4 + l, at, :] * (v[c] - v[c - 4])
                a, acc[c - 4] = a + f, acc[c - 4] - f
            if i:
                f = gx[c - 16, at, :] * (v[c] - v.pop(c - 16))
                a = a + f
                emit(c - 16, acc.pop(c - 16) - f)
            acc[c] = a
        for c in range(48, 64):
            emit(c, acc[c])

    def send(r, feats):
        n = sum(f.shape[0] for f in feats)
        full = jnp.concatenate(list(feats) + [jnp.zeros((128 - n, 128), F32)], axis=0)
        snd[r] = full.T
        rcv[r, pl.ds(me, 1), :] = snd[r, pl.ds(me, 1), :]
        for px, py, p in others:
            pltpu.make_async_remote_copy(
                src_ref=snd.at[r, pl.ds(p, 1)], dst_ref=rcv.at[r, pl.ds(me, 1)],
                send_sem=ssem.at[r], recv_sem=rsem.at[r], device_id=(px, py), device_id_type=MESH,
            ).start()

    def receive(r):
        all_of(r).wait_recv()
        return rcv[r].T

    def total(rows):
        return jnp.sum(rows, axis=1, keepdims=True)

    def same_cell():
        key = jnp.where(celltab[...] >= 0, celltab[...] * 128 + lanetab[...], -1).astype(F32)
        kept[...] = key.T
        keys[...] = key

        def one(b, c):
            cols = []
            for h in range(2):
                hit = iota((128, 64), 1) == b + 32 * h
                cols.append(jnp.sum(jnp.where(hit, kept[...], 0.0), axis=1, keepdims=True))
            for h in range(2):
                row = keys[pl.ds(b + 32 * h, 1), :]
                n = jnp.zeros((1, 128), F32)
                for g in range(2):
                    n = n + jnp.sum(jnp.where(cols[g] == row, 1.0, 0.0), axis=0, keepdims=True)
                slots2[pl.ds(b + 32 * h, 1), :] = jnp.where(n > 1.5, 1.0, 0.0)
            return c

        lax.fori_loop(0, 32, one, 0)
        shared = to_entries(slots2).astype(BF16)
        rows_before = dot_nn((iota((32, 32), 1) < iota((32, 32), 0)).astype(F32).astype(BF16), shared)
        at = dot_nn(shared, tri) + dot_nn(rows_before.astype(BF16), ones) - 1.0
        at = jnp.where(shared.astype(F32) > 0.5, at, -1.0)
        most = jnp.max(jnp.max(at, axis=0, keepdims=True), axis=1, keepdims=True)
        at = at.astype(I32)
        place_of[...] = at
        acc = jnp.zeros((16, 128), F32)
        for i in range(32):
            hit = (iota((128, 128), 0) == at[i : i + 1]).astype(F32).astype(BF16)
            row = fc[i : i + 1]
            vals = [jnp.full((1, 128), i + 1, I32), iota((1, 128), 1), row >> 12, (row >> 7) & 31, row & 127]
            vals = jnp.concatenate(vals + [jnp.zeros((11, 128), I32)], axis=0)
            acc = acc + dot_nt(vals.astype(F32).astype(BF16), hit)
        list_row[...] = jnp.broadcast_to(acc[0:1].astype(I32) - 1, (8, 128))
        list_lane[...] = jnp.broadcast_to(acc[1:2].astype(I32), (8, 128))
        name = acc[2:3] * 4096.0 + acc[3:4] * 128.0 + acc[4:5]
        name = jnp.broadcast_to(jnp.where(acc[0:1] > 0.5, name, -1.0), (128, 128))
        other = iota((128, 128), 0) != iota((128, 128), 1)
        same = jnp.logical_and(jnp.logical_and(name == name.T, name >= 0.0), other)
        mates[...] = jnp.where(same, 1.0, 0.0).astype(BF16)
        return jnp.where(most > 127.5, 1.0, 0.0)

    def joined(f):
        got = jnp.zeros((8, 128), F32)
        for g in range(4):
            v = lanes_of(f[8 * g : 8 * g + 8, :], list_lane[...])
            got = got + jnp.where(list_row[...] == iota((8, 128), 0) + 8 * g, v, 0.0)
        got = jnp.sum(got, axis=0, keepdims=True)
        p0 = got.astype(BF16).astype(F32)
        p1 = (got - p0).astype(BF16).astype(F32)
        p = jnp.concatenate([p0, p1, got - p0 - p1, jnp.zeros((13, 128), F32)], axis=0).astype(BF16)
        o = dot_nn(p, mates[...])
        more = jnp.broadcast_to((o[0:1] + o[1:2]) + o[2:3], (8, 128))
        outs = []
        for g in range(4):
            at = place_of[8 * g : 8 * g + 8, :]
            v = lanes_of(more, jnp.maximum(at, 0) & 127)
            outs.append(f[8 * g : 8 * g + 8, :] + jnp.where(at >= 0, v, 0.0))
        return jnp.concatenate(outs, axis=0)

    def dot_all(v):
        return jnp.sum(jnp.sum(v, axis=0, keepdims=True), axis=1, keepdims=True)

    def spread(v):
        return jnp.broadcast_to(v, (8, 128))

    zero = jnp.zeros((8, 128), F32)
    gather(kf, slots)
    gather(xf, slots2)
    k_own, t_own = to_entries(slots), to_entries(slots2)
    wo[...] = k_own
    zo[...] = t_own
    round0 = [k_own, t_own, ids]
    pl.semaphore_wait(barrier, 127)
    lrcv[pl.ds(me, 1)] = lsnd[pl.ds(me, 1)]
    for n, (px, py, p) in enumerate(others):
        if n == 48:
            send(0, round0)
        pltpu.make_async_remote_copy(
            src_ref=lsnd.at[pl.ds(p, 1)], dst_ref=lrcv.at[pl.ds(me, 1)],
            send_sem=lssem, recv_sem=lrsem, device_id=(px, py), device_id_type=MESH,
        ).start()
    many = same_cell()
    msgs[...] = receive(0)
    gface[...] = area[...] * 0.5 * (wo[...] + msgs[0:32, :])
    flows[...] = gface[...] * (zo[...] - msgs[32:64, :])
    to_slots(flows, slots)
    scatter(slots)
    tids = msgs[64:72, :].astype(I32)
    for j in range(8):
        oht[:, pl.ds(128 * j, 128)] = (iota((1024, 128), 0) == tids[j : j + 1]).astype(F32).astype(BF16)

    def first(k, c):
        at = pl.ds(8 * k, 8)

        def emit(c, a):
            rb[c, at, :] = a + nat[pl.ds(512 * k + c, 8, stride=64), :]

        stencil(k, lambda c: xf[c, at, :], emit, False)
        return c

    lax.fori_loop(0, 4, first, 0)
    laser().wait_recv()
    by_rank = []
    for j in range(8):
        by_rank.append(lrcv[:, j, :])
    pieces = thirds(jnp.concatenate(by_rank, axis=0))
    for q in range(8):
        o = oht[pl.ds(128 * q, 128), :]
        h = (dot_nn(o, pieces[0]) + dot_nn(o, pieces[1])) + dot_nn(o, pieces[2])
        for part in range(4):
            heat[pl.ds(512 * q + part, 128, stride=4), :] = h[:, 64 * part : 64 * part + 64]
        for b in range(4 * q, 4 * q + 4):
            en[64 * b : 64 * b + 64, :] = heat[128 * b : 128 * b + 128, :].T

    def start(k, c):
        at = pl.ds(8 * k, 8)
        for c in range(64):
            ra[c, at, :] = en[pl.ds(512 * k + c, 8, stride=64), :] - rb[c, at, :]
        return 0

    lax.fori_loop(0, 4, start, 0)
    gather(ra, slots2)
    ro[...] = to_entries(slots2)
    send(1, [ro[...], spread(jnp.maximum(over, many))])

    def early(k, sums):
        at = pl.ds(8 * k, 8)
        s = list(sums)

        def emit(c, a):
            r = ra[c, at, :]
            wf[c, at, :] = a
            s[0] = s[0] + r * r
            s[1] = s[1] + r * a

        stencil(k, lambda c: ra[c, at, :], emit, True)
        return tuple(s)

    rr, rw = [dot_all(v) for v in lax.fori_loop(0, 4, early, (zero, zero))]
    gather(wf, slots2)
    wo[...] = to_entries(slots2)
    msgs[...] = receive(1)
    flag_out[...] = jnp.max(msgs[32:33, :], axis=1, keepdims=True)
    flux = gface[...] * (ro[...] - msgs[0:32, :])
    flows[...] = flux
    rw = rw + dot_all(ro[...] * flux)
    wo[...] = wo[...] + joined(flux)

    old_rr = old_alpha = alpha1 = beta1 = None
    r_now, r_next = ra, rb
    for it in range(ITERS):
        last = it == ITERS - 1
        if last:
            send(it + 2, [spread(rr), spread(rw)])
        else:
            send(it + 2, [wo[...], spread(rr), spread(rw)])
        to_slots(flows, slots)
        scatter(slots)
        if it:
            r_now, r_next = r_next, r_now
            alpha, beta = spread(alpha1), None if it == 1 else spread(beta1)

        def along(k, sums, it=it, last=last, r_now=r_now, r_next=r_next):
            at = pl.ds(8 * k, 8)
            d = list(sums)

            def load(c):
                here = nat[pl.ds(512 * k + c, 8, stride=64), :]
                if it == 0:
                    w = wf[c, at, :] + here
                    wf[c, at, :] = w
                    d[2] = d[2] + w * w
                    return w
                w = wf[c, at, :]
                z = uf[c, at, :] + here
                s = w
                r = r_next[c, at, :]
                q = r
                if it > 1:
                    z = z + beta * zf[c, at, :]
                    s = s + beta * sf[c, at, :]
                    q = q + beta * pf[c, at, :]
                pf[c, at, :] = q
                xf[c, at, :] = xf[c, at, :] + alpha * q
                sf[c, at, :] = s
                r = r - alpha * s
                w = w - alpha * z
                r_now[c, at, :] = r
                wf[c, at, :] = w
                if not last:
                    zf[c, at, :] = z
                    for n, (p, q) in enumerate(((r, r), (r, w), (w, w), (r, s), (w, s), (s, s), (w, z), (s, z))):
                        d[n] = d[n] + p * q
                return w

            def emit(c, a):
                uf[c, at, :] = a
                d[8] = d[8] + wf[c, at, :] * a

            if last:
                for c in range(64):
                    load(c)
            else:
                stencil(k, load, emit, True)
            return tuple(d)

        dots = lax.fori_loop(0, 4, along, (zero,) * 9)
        if last:
            outs = [
                pltpu.make_async_copy(src, dst, out_sem.at[n])
                for n, (src, dst) in enumerate(zip((xf, r_now, pf, wf, sf), (x_out, r_out, p_out, w_out, s_out)))
            ]
            for c in outs:
                c.start()
        else:
            dots = [dot_all(v) for v in dots]
            if it == 0:
                dots[0], dots[1] = rr, rw
            gather(uf, slots2)
            ro[...] = to_entries(slots2)
        msgs[...] = receive(it + 2)
        base = 0 if last else 32
        g_rr, g_rw = total(msgs[base : base + 1, :]), total(msgs[base + 8 : base + 9, :])
        if it:
            beta1 = g_rr / old_rr
            alpha1 = g_rr / (g_rw - beta1 * g_rr / old_alpha)
        else:
            alpha1 = g_rr / g_rw
        old_rr, old_alpha = g_rr, alpha1
        if last:
            break
        flux = gface[...] * (wo[...] - msgs[0:32, :])
        flows[...] = flux
        rr, rw, ww, rs, ws, ss, wz, sz, wu = dots
        wq = wu + dot_all(wo[...] * flux)
        z = ro[...] + joined(flux)
        s = wo[...]
        if it:
            z = z + beta1 * zo[...]
            rs = rw + beta1 * rs
            ss = ww + beta1 * (2.0 * ws + beta1 * ss)
            sz = wq + beta1 * (2.0 * wz + beta1 * sz)
            ws = ww + beta1 * ws
        else:
            rs, ss, sz, ws = rw, ww, wq, ww
        zo[...] = z
        wo[...] = s - alpha1 * z
        rr = rr + alpha1 * (alpha1 * ss - 2.0 * rs)
        rw = rw + alpha1 * (alpha1 * sz - 2.0 * ws)

    scale_out[0:8, :] = spread(alpha1)
    scale_out[8:16, :] = spread(beta1)
    for r in range(ROUNDS):
        all_of(r).wait_send()
    laser().wait_send()
    for c in outs:
        c.wait()


def finish_kernel(scale, x, r, p, w, s, x_out, r_out):
    alpha, beta = scale[0:8, :], scale[8:16, :]
    for c in range(16):
        for k in range(4):
            at, to = pl.ds(8 * k, 8), pl.ds(64 * k + c % 8, 8, stride=8)
            x_out[c // 8, to, :] = x[c, at, :] + alpha * (r[c, at, :] + beta * p[c, at, :])
            r_out[c // 8, to, :] = r[c, at, :] - alpha * (w[c, at, :] + beta * s[c, at, :])


def finish(scale, *fields):
    of = pl.BlockSpec((16, 32, 128), lambda k: (k, 0, 0))
    to = pl.BlockSpec((2, 256, 128), lambda k: (k, 0, 0))
    x, r = pl.pallas_call(
        finish_kernel,
        grid=(4,),
        out_shape=[jax.ShapeDtypeStruct((8, 256, 128), F32)] * 2,
        in_specs=[pl.BlockSpec((16, 128), lambda k: (0, 0))] + [of] * 5,
        out_specs=[to] * 2,
    )(scale, *fields)
    return untiled(x), untiled(r)


def tiled(v):
    return v.reshape(8, 8, 32, 128).transpose(0, 2, 1, 3).reshape(2048, 128)


def untiled(v):
    return v.reshape(8, 32, 8, 128).transpose(0, 2, 1, 3).reshape(64, 4096)


def vm(*shape, dtype=F32):
    return pltpu.VMEM(shape, dtype)


def shards(*args):
    temp, base, store, level, face, area, rows, owner, tile = args
    field = lambda: vm(64, 32, 128)
    part = lambda: vm(48, 32, 128)
    slot = lambda dtype=F32: vm(64, 128, dtype=dtype)
    *fields, flag, scale = pl.pallas_call(
        step_kernel,
        out_shape=[
            *[jax.ShapeDtypeStruct((64, 32, 128), F32)] * 5,
            jax.ShapeDtypeStruct((1, 1), F32),
            jax.ShapeDtypeStruct((16, 128), F32),
        ],
        in_specs=[pl.BlockSpec(memory_space=pl.ANY)] * 9,
        out_specs=[pl.BlockSpec(memory_space=pl.ANY)] * 5 + [pl.BlockSpec(memory_space=pltpu.VMEM)] * 2,
        scratch_shapes=[
            vm(2048, 128), vm(2048, 128), vm(2048, 128),
            vm(32, 128, dtype=I32), vm(32, 128, dtype=I32), vm(32, 128), vm(256, 256),
            vm(1, 256, dtype=I32), vm(1, 256, dtype=I32),
            field(), field(), field(), part(), part(), part(),
            field(), field(), field(), field(), field(), vm(2048, 128), vm(2048, 128),
            vm(1024, 128, dtype=BF16), vm(32, 128, 256, dtype=BF16),
            slot(I32), slot(I32), slot(I32), slot(I32), vm(32, 128, dtype=I32), vm(32, 128, dtype=I32),
            slot(), slot(), vm(128, 128),
            vm(32, 128), vm(32, 128), vm(32, 128), vm(32, 128), vm(32, 128), vm(4096, 64), vm(1024, 1024, dtype=BF16),
            field(), field(), vm(128, 64), slot(), vm(32, 128, dtype=I32), vm(8, 128, dtype=I32), vm(8, 128, dtype=I32), vm(128, 128, dtype=BF16),
            vm(ROUNDS, 128, 128), vm(ROUNDS, 128, 128), vm(128, 8, 256), vm(128, 8, 256),
            pltpu.SemaphoreType.DMA((9,)),
            pltpu.SemaphoreType.DMA((ROUNDS,)),
            pltpu.SemaphoreType.DMA((ROUNDS,)),
            pltpu.SemaphoreType.DMA,
            pltpu.SemaphoreType.DMA,
            pltpu.SemaphoreType.DMA((5,)),
        ],
        compiler_params=pltpu.CompilerParams(
            collective_id=0, has_side_effects=True, vmem_limit_bytes=63 * 1024 * 1024
        ),
    )(
        tiled(temp), tiled(base), tiled(store), level.reshape(32, 128),
        face[0].T, area[0].T, rows[0], owner.reshape(1, 256), tile,
    )
    return lax.cond(
        flag[0, 0] > 0.5,
        lambda: general(*args),
        lambda: finish(scale, *fields),
    )


def solution(mesh):
    return jax.shard_map(
        shards,
        mesh=mesh,
        in_specs=(
            P(None, ("bx", "by")),
            P(None, ("bx", "by")),
            P(None, ("bx", "by")),
            P(("bx", "by")),
            P(("bx", "by"), None, None),
            P(("bx", "by"), None, None),
            P(None, ("bx", "by"), None),
            P(None, ("bx", "by"), None),
            P(None, ("bx", "by")),
        ),
        out_specs=(P(None, ("bx", "by")), P(None, ("bx", "by"))),
        check_vma=False,
    )
```

```python
import functools

import jax
import jax.numpy as jnp
from jax import lax
from jax.experimental import pallas as pl
from jax.experimental.pallas import tpu as pltpu
from jax.sharding import PartitionSpec as P

CAP = 8
ITERS = 4
MESH = pl.DeviceIdType.MESH
F32, BF16, I32 = jnp.float32, jnp.bfloat16, jnp.int32
ROUNDS = 6


def cond_links(diffuse_warmth, spacing):
    grid_cube = diffuse_warmth.reshape(4, 4, 4, -1)
    first_pairs = spacing * 0.5 * (grid_cube[1:] + grid_cube[:-1])
    second_pairs = spacing * 0.5 * (grid_cube[:, 1:] + grid_cube[:, :-1])
    third_pairs = spacing * 0.5 * (grid_cube[:, :, 1:] + grid_cube[:, :, :-1])
    return (first_pairs, second_pairs, third_pairs)


def inside_energy_current(values, interface_couplings):
    grid_cube = values.reshape(4, 4, 4, -1)
    flux_one = interface_couplings[0] * (grid_cube[1:] - grid_cube[:-1])
    flux_two = interface_couplings[1] * (grid_cube[:, 1:] - grid_cube[:, :-1])
    flux_three = interface_couplings[2] * (grid_cube[:, :, 1:] - grid_cube[:, :, :-1])
    zero_pad = (0, 0)
    balance = jnp.pad(flux_one, ((1, 0), zero_pad, zero_pad, zero_pad)) - jnp.pad(
        flux_one, ((0, 1), zero_pad, zero_pad, zero_pad)
    )
    balance = (
        balance
        + jnp.pad(flux_two, (zero_pad, (1, 0), zero_pad, zero_pad))
        - jnp.pad(flux_two, (zero_pad, (0, 1), zero_pad, zero_pad))
    )
    balance = (
        balance
        + jnp.pad(flux_three, (zero_pad, zero_pad, (1, 0), zero_pad))
        - jnp.pad(flux_three, (zero_pad, zero_pad, (0, 1), zero_pad))
    )
    return balance.reshape(values.shape)


def interface_energy_current(values, voxel_lattice, interface_diffusivity, own_vals, peer_vals):
    flux_vals = interface_diffusivity * (own_vals - peer_vals)
    flat_zero = jnp.zeros((values.size,), jnp.float32)
    return flat_zero.at[voxel_lattice.reshape(-1)].add(flux_vals.reshape(-1)).reshape(values.shape)


def apply_operator(values, heat_mass, interface_couplings, voxel_lattice, interface_diffusivity):
    own_vals = values.reshape(-1)[voxel_lattice]
    peer_vals = lax.all_to_all(own_vals, ("bx", "by"), split_axis=0, concat_axis=0, tiled=True)
    return (
        heat_mass * values
        + inside_energy_current(values, interface_couplings)
        + interface_energy_current(
            values, voxel_lattice, interface_diffusivity, own_vals, peer_vals
        )
    )


def squares(values):
    return lax.psum(jnp.sum(values * values), ("bx", "by"))


def general(
    initial_thermal_state,
    baseline_diffusivity,
    thermal_storage,
    refinement_depth,
    interface_voxel_table,
    interface_weighting,
    laser_energy_deposits,
    laser_spot_holder,
    laser_spot_patch,
):
    owner_count = lax.axis_size(("bx", "by"))
    voxel_lattice = interface_voxel_table[0]
    areas = interface_weighting[0]
    patch_number = initial_thermal_state.shape[1] // 4
    step_count = laser_energy_deposits.shape[0]
    row_width = laser_energy_deposits.shape[2]
    spacing = 0.5 ** refinement_depth.astype(jnp.float32)
    heat_mass = thermal_storage * spacing**3

    def bucket(owners, tiles, row_block):
        matches = (owners[:, None] == jnp.arange(owner_count, dtype=jnp.int32)[None, :]).astype(
            jnp.int32
        )
        slot_rank = jnp.sum((jnp.cumsum(matches, 0) - 1) * matches, 1)
        slot_dest = owners * CAP + slot_rank
        sent_rows = (
            jnp.zeros((owner_count * CAP, row_width), jnp.float32).at[slot_dest].set(row_block)
        )
        sent_ids = (
            jnp.full((owner_count * CAP,), -1.0, jnp.float32)
            .at[slot_dest]
            .set(tiles.astype(jnp.float32))
        )
        return (sent_rows.reshape(owner_count, CAP, row_width), sent_ids.reshape(owner_count, CAP))

    sent_rows, sent_ids = jax.vmap(bucket)(
        laser_spot_holder[:, :, 0], laser_spot_patch, laser_energy_deposits
    )
    got_rows, got_ids = (
        lax.all_to_all(sent_rows, ("bx", "by"), split_axis=1, concat_axis=1, tiled=True),
        lax.all_to_all(sent_ids, ("bx", "by"), split_axis=1, concat_axis=1, tiled=True),
    )
    got_rows = got_rows.reshape(step_count, -1, row_width)
    got_ids = got_ids.reshape(step_count, -1)
    tile_iota = jnp.arange(patch_number, dtype=jnp.float32)
    equation_misfit = jnp.zeros_like(initial_thermal_state)
    matches = (got_ids[0][None, :] == tile_iota[:, None]).astype(jnp.float32)
    tile_heat = jnp.dot(
        matches, got_rows[0], precision=lax.Precision.HIGHEST, preferred_element_type=jnp.float32
    )
    energy_input = jnp.transpose(tile_heat.reshape(patch_number, 4, 64), (2, 0, 1)).reshape(
        64, patch_number * 4
    )
    diffuse_warmth = baseline_diffusivity * (1.0 + 0.5 * jnp.tanh(initial_thermal_state))
    interface_couplings = cond_links(diffuse_warmth, spacing)
    own_k = diffuse_warmth.reshape(-1)[voxel_lattice]
    home_thermal_state = initial_thermal_state.reshape(-1)[voxel_lattice]
    peer_k = lax.all_to_all(own_k, ("bx", "by"), split_axis=0, concat_axis=0, tiled=True)
    neighbor_thermal_state = lax.all_to_all(
        home_thermal_state, ("bx", "by"), split_axis=0, concat_axis=0, tiled=True
    )
    interface_diffusivity = areas * 0.5 * (own_k + peer_k)
    equation_misfit = energy_input - (
        inside_energy_current(initial_thermal_state, interface_couplings)
        + interface_energy_current(
            initial_thermal_state,
            voxel_lattice,
            interface_diffusivity,
            home_thermal_state,
            neighbor_thermal_state,
        )
    )
    conjugate_gradient_loop = initial_thermal_state

    def one_turn(turn_index, carry):
        conjugate_gradient_loop, equation_misfit, direction, res_norm = carry
        applied = apply_operator(
            direction, heat_mass, interface_couplings, voxel_lattice, interface_diffusivity
        )
        step_size = res_norm / lax.psum(jnp.sum(direction * applied), ("bx", "by"))
        conjugate_gradient_loop = conjugate_gradient_loop + step_size * direction
        equation_misfit = equation_misfit - step_size * applied
        next_norm = squares(equation_misfit)
        direction = equation_misfit + next_norm / res_norm * direction
        return (conjugate_gradient_loop, equation_misfit, direction, next_norm)

    start_norm = squares(equation_misfit)
    carry = one_turn(0, (conjugate_gradient_loop, equation_misfit, equation_misfit, start_norm))
    conjugate_gradient_loop, equation_misfit, direction, start_norm = lax.fori_loop(1, ITERS, one_turn, carry)
    return (conjugate_gradient_loop, equation_misfit)


def lanes_of(x, idx):
    return jnp.take_along_axis(x, idx, axis=1, mode="promise_in_bounds")


def thirds(x):
    a = x.astype(BF16)
    rest = x - a.astype(F32)
    b = rest.astype(BF16)
    c = (rest - b.astype(F32)).astype(BF16)
    return a, b, c


def iota(shape, dim):
    return lax.broadcasted_iota(I32, shape, dim)


def dot_nt(a, b):
    return lax.dot_general(a, b, (((1,), (1,)), ((), ())), preferred_element_type=F32)


def dot_nn(a, b):
    return jnp.dot(a, b, preferred_element_type=F32)


def peers():
    bx, by = lax.axis_index("bx"), lax.axis_index("by")
    offs = []
    for dc in range(2):
        for dy in range(4):
            for dx in range(4):
                for dz in range(4):
                    if (dc, dy, dx, dz) != (0, 0, 0, 0):
                        hops = min(dy, 4 - dy) + min(dx, 4 - dx) + min(dz, 4 - dz)
                        offs.append((-hops, dc, dy, dx, dz))
    offs.sort()
    y, core, x, z = bx // 2, lax.rem(bx, 2), by // 4, lax.rem(by, 4)
    ys = [lax.rem(y + d, 4) * 2 for d in range(4)]
    cores = [lax.rem(core + d, 2) for d in range(2)]
    xs = [lax.rem(x + d, 4) * 4 for d in range(4)]
    zs = [lax.rem(z + d, 4) for d in range(4)]
    pxs = [[ys[d] + cores[e] for e in range(2)] for d in range(4)]
    pys = [[xs[d] + zs[e] for e in range(4)] for d in range(4)]
    return [(pxs[dy][dc], pys[dx][dz], pxs[dy][dc] * 16 + pys[dx][dz]) for _, dc, dy, dx, dz in offs]


def step_kernel(
    temp_hbm, base_hbm, store_hbm, level_hbm, face_hbm, area_hbm, rows_hbm, owner_hbm, tile_hbm,
    x_out, r_out, p_out, w_out, s_out, flag_out, scale_out,
    in_t, in_b, in_s, level, face, area, rows, owner, tile,
    xf, kf, mf, gx, gy, gz, ra, rb, wf, sf, pf, nat, en,
    ohs, ohl, celltab, lanetab, srcrow, srclane, rowid, slane, slots, slots2, msgs,
    ro, wo, zo, gface, flows, heat, oht, uf, zf, kept, keys, place_of, list_row, list_lane, mates,
    snd, rcv, lsnd, lrcv,
    in_sem, ssem, rsem, lssem, lrsem, out_sem,
):
    bx, by = lax.axis_index("bx"), lax.axis_index("by")
    me = bx * 16 + by
    barrier = pltpu.get_barrier_semaphore()
    def laser():
        return pltpu.make_async_remote_copy(
            src_ref=lsnd.at[pl.ds(0, 127)], dst_ref=lrcv.at[pl.ds(0, 127)],
            send_sem=lssem, recv_sem=lrsem, device_id=(lax.rem(bx + 1, 8), by), device_id_type=MESH,
        )

    def all_of(r):
        return pltpu.make_async_remote_copy(
            src_ref=snd.at[r, pl.ds(0, 127)], dst_ref=rcv.at[r, pl.ds(0, 127)],
            send_sem=ssem.at[r], recv_sem=rsem.at[r],
            device_id=(lax.rem(bx + 1, 8), by), device_id_type=MESH,
        )
    others = peers()
    for px, py, _ in others:
        pl.semaphore_signal(barrier, inc=1, device_id=(px, py), device_id_type=MESH)

    loads = [
        pltpu.make_async_copy(src, dst, in_sem.at[i])
        for i, (src, dst) in enumerate(
            [(owner_hbm, owner), (tile_hbm, tile), (rows_hbm, rows), (face_hbm, face), (area_hbm, area), (level_hbm, level),
             (temp_hbm, in_t), (base_hbm, in_b), (store_hbm, in_s)]
        )
    ]
    for c in loads:
        c.start()

    for c in loads[:3]:
        c.wait()
    own = owner[...]
    match = iota((128, 256), 0) == own
    upto = (iota((256, 256), 0) <= iota((256, 256), 1)).astype(F32).astype(BF16)
    before = dot_nn(match.astype(F32).astype(BF16), upto) - 1.0
    rank = jnp.sum(jnp.where(match, before, 0.0), axis=0, keepdims=True)
    dest = own * CAP + rank.astype(I32)
    place = (iota((1024, 256), 0) == dest).astype(F32).astype(BF16)
    pieces = thirds(rows[...])
    put = (dot_nn(place, pieces[0]) + dot_nn(place, pieces[1])) + dot_nn(place, pieces[2])
    lsnd[...] = put.reshape(128, 8, 256)
    num = tile[...] + 1
    is_rank = iota((8, 256), 0) == rank.astype(I32)
    high = jnp.where(is_rank, num >> 5, 0).astype(F32)
    low = jnp.where(is_rank, num & 31, 0).astype(F32)
    hl = jnp.concatenate([high, low], axis=0).astype(BF16)
    ids = dot_nt(hl, match.astype(F32).astype(BF16))
    ids = ids[0:8] * 32.0 + ids[8:16] - 1.0

    for c in loads[3:6]:
        c.wait()
    fc = face[...]
    bt = (fc & 4095) >> 7
    for i in range(32):
        ohs[pl.ds(32 * i, 32), :] = (iota((32, 128), 0) == bt[i : i + 1]).astype(F32).astype(BF16)
    tri = (iota((128, 128), 0) <= iota((128, 128), 1)).astype(F32).astype(BF16)
    ones = jnp.ones((128, 128), BF16)
    run = jnp.zeros((32, 128), F32)
    ranks = []
    for i in range(32):
        oh = ohs[pl.ds(32 * i, 32), :]
        pre = dot_nn(oh, tri)
        ranks.append(jnp.sum(oh.astype(F32) * (pre + run - 1.0), axis=0, keepdims=True))
        run = run + dot_nn(oh, ones)
    rank = jnp.concatenate(ranks, axis=0).astype(I32)
    over = jnp.max(jnp.max((rank >= 256).astype(F32), axis=0, keepdims=True), axis=1, keepdims=True)
    rid = (rank >> 7) * 32 + bt
    rowid[...] = rid
    slane[...] = rank & 127
    cellv = (fc >> 12).astype(F32)
    lanev = (fc & 127).astype(F32)
    lane_f = iota((1, 128), 1).astype(F32)
    acc = jnp.zeros((256, 128), F32)
    for i in range(32):
        hit = iota((64, 128), 0) == rid[i : i + 1]
        a = jnp.concatenate(
            [
                jnp.where(hit, F32(i + 1), 0.0),
                jnp.where(hit, lane_f, 0.0),
                jnp.where(hit, cellv[i : i + 1], 0.0),
                jnp.where(hit, lanev[i : i + 1], 0.0),
            ],
            axis=0,
        ).astype(BF16)
        b = (iota((128, 128), 0) == slane[i : i + 1, :]).astype(F32).astype(BF16)
        acc = acc + dot_nt(a, b)
    tab = acc.astype(I32)
    filled = tab[0:64] > 0
    srcrow[...] = tab[0:64] - 1
    srclane[...] = tab[64:128]
    celltab[...] = jnp.where(filled, tab[128:192], -1)
    lanetab[...] = tab[192:256]

    def lane_hot(b, c):
        for h in range(2):
            row = lanetab[pl.ds(b + 32 * h, 1), :]
            ohl[pl.ds(b, 1), :, pl.ds(128 * h, 128)] = (
                (iota((128, 128), 0) == row).astype(F32).astype(BF16).reshape(1, 128, 128)
            )
        return c

    lax.fori_loop(0, 32, lane_hot, 0)

    for c in loads[6:]:
        c.wait()

    def prepare(k, c):
        lv = level[pl.ds(8 * k, 8), :]
        spacing = jnp.where(lv == 0, 1.0, jnp.where(lv == 1, 0.5, 0.25)).astype(F32)
        cube = spacing * spacing * spacing
        half = spacing * 0.5
        at = pl.ds(8 * k, 8)
        kv = {}
        for c in range(64):
            i, j, l = c // 16, (c // 4) % 4, c % 4
            where = pl.ds((c // 8) * 256 + c % 8 + 64 * k, 8, stride=8)
            t = in_t[where, :]
            kc = in_b[where, :] * (1.0 + 0.5 * jnp.tanh(t))
            xf[c, at, :] = t
            kf[c, at, :] = kc
            mf[c, at, :] = in_s[where, :] * cube
            kv[c] = kc
            if i:
                gx[c - 16, at, :] = half * (kc + kv.pop(c - 16))
            if j:
                gy[(i * 3 + j - 1) * 4 + l, at, :] = half * (kc + kv[c - 4])
            if l:
                gz[(i * 4 + j) * 3 + l - 1, at, :] = half * (kc + kv[c - 1])
        return 0

    lax.fori_loop(0, 4, prepare, 0)

    def gather(field, out):
        def group(k, c):
            at, at2 = pl.ds(8 * k, 8), pl.ds(32 + 8 * k, 8)
            l0, l1, c0, c1 = lanetab[at, :], lanetab[at2, :], celltab[at, :], celltab[at2, :]
            a0 = jnp.zeros((8, 128), F32)
            a1 = jnp.zeros((8, 128), F32)
            for cell in range(64):
                v = field[cell, at, :]
                a0 = jnp.where(c0 == cell, lanes_of(v, l0), a0)
                a1 = jnp.where(c1 == cell, lanes_of(v, l1), a1)
            out[at, :] = a0
            out[at2, :] = a1
            return c

        lax.fori_loop(0, 4, group, 0)

    def to_entries(src):
        outs = []
        for g in range(4):
            ri, la = rowid[8 * g : 8 * g + 8, :], slane[8 * g : 8 * g + 8, :]
            a = jnp.zeros((8, 128), F32)
            for t in range(64):
                row = jnp.broadcast_to(src[t : t + 1, :], (8, 128))
                a = jnp.where(ri == t, lanes_of(row, la), a)
            outs.append(a)
        return jnp.concatenate(outs, axis=0)

    def to_slots(src, out):
        for g in range(8):
            ri, la = srcrow[8 * g : 8 * g + 8, :], srclane[8 * g : 8 * g + 8, :]
            a = jnp.zeros((8, 128), F32)
            for t in range(32):
                row = jnp.broadcast_to(src[t : t + 1, :], (8, 128))
                a = jnp.where(ri == t, lanes_of(row, la), a)
            out[8 * g : 8 * g + 8, :] = a

    def scatter(flux):
        def one(b, c):
            parts = [[], [], []]
            for h in range(2):
                row = flux[pl.ds(b + 32 * h, 1), :]
                hit = iota((64, 128), 0) == celltab[pl.ds(b + 32 * h, 1), :]
                p0 = row.astype(BF16).astype(F32)
                p1 = (row - p0).astype(BF16).astype(F32)
                p2 = row - p0 - p1
                for q, p in enumerate((p0, p1, p2)):
                    parts[q].append(jnp.where(hit, p, 0.0))
            a = jnp.concatenate([jnp.concatenate(p, axis=1) for p in parts], axis=0).astype(BF16)
            o = dot_nt(a, ohl[b])
            nat[pl.ds(64 * b, 64), :] = (o[0:64] + o[64:128]) + o[128:192]
            return c

        lax.fori_loop(0, 32, one, 0, unroll=32)

    def stencil(k, load, emit, mass):
        at = pl.ds(8 * k, 8)
        v, acc = {}, {}
        for c in range(64):
            i, j, l = c // 16, (c // 4) % 4, c % 4
            v[c] = load(c)
            a = mf[c, at, :] * v[c] if mass else jnp.zeros((8, 128), F32)
            if l:
                f = gz[(i * 4 + j) * 3 + l - 1, at, :] * (v[c] - v[c - 1])
                a, acc[c - 1] = a + f, acc[c - 1] - f
            if j:
                f = gy[(i * 3 + j - 1) * 4 + l, at, :] * (v[c] - v[c - 4])
                a, acc[c - 4] = a + f, acc[c - 4] - f
            if i:
                f = gx[c - 16, at, :] * (v[c] - v.pop(c - 16))
                a = a + f
                emit(c - 16, acc.pop(c - 16) - f)
            acc[c] = a
        for c in range(48, 64):
            emit(c, acc[c])

    def send(r, feats):
        n = sum(f.shape[0] for f in feats)
        full = jnp.concatenate(list(feats) + [jnp.zeros((128 - n, 128), F32)], axis=0)
        snd[r] = full.T
        rcv[r, pl.ds(me, 1), :] = snd[r, pl.ds(me, 1), :]
        for px, py, p in others:
            pltpu.make_async_remote_copy(
                src_ref=snd.at[r, pl.ds(p, 1)], dst_ref=rcv.at[r, pl.ds(me, 1)],
                send_sem=ssem.at[r], recv_sem=rsem.at[r], device_id=(px, py), device_id_type=MESH,
            ).start()

    def receive(r):
        all_of(r).wait_recv()
        return rcv[r].T

    def total(rows):
        return jnp.sum(rows, axis=1, keepdims=True)

    def same_cell():
        key = jnp.where(celltab[...] >= 0, celltab[...] * 128 + lanetab[...], -1).astype(F32)
        kept[...] = key.T
        keys[...] = key

        def one(b, c):
            cols = []
            for h in range(2):
                hit = iota((128, 64), 1) == b + 32 * h
                cols.append(jnp.sum(jnp.where(hit, kept[...], 0.0), axis=1, keepdims=True))
            for h in range(2):
                row = keys[pl.ds(b + 32 * h, 1), :]
                n = jnp.zeros((1, 128), F32)
                for g in range(2):
                    n = n + jnp.sum(jnp.where(cols[g] == row, 1.0, 0.0), axis=0, keepdims=True)
                slots2[pl.ds(b + 32 * h, 1), :] = jnp.where(n > 1.5, 1.0, 0.0)
            return c

        lax.fori_loop(0, 32, one, 0)
        shared = to_entries(slots2).astype(BF16)
        rows_before = dot_nn((iota((32, 32), 1) < iota((32, 32), 0)).astype(F32).astype(BF16), shared)
        at = dot_nn(shared, tri) + dot_nn(rows_before.astype(BF16), ones) - 1.0
        at = jnp.where(shared.astype(F32) > 0.5, at, -1.0)
        most = jnp.max(jnp.max(at, axis=0, keepdims=True), axis=1, keepdims=True)
        at = at.astype(I32)
        place_of[...] = at
        acc = jnp.zeros((16, 128), F32)
        for i in range(32):
            hit = (iota((128, 128), 0) == at[i : i + 1]).astype(F32).astype(BF16)
            row = fc[i : i + 1]
            vals = [jnp.full((1, 128), i + 1, I32), iota((1, 128), 1), row >> 12, (row >> 7) & 31, row & 127]
            vals = jnp.concatenate(vals + [jnp.zeros((11, 128), I32)], axis=0)
            acc = acc + dot_nt(vals.astype(F32).astype(BF16), hit)
        list_row[...] = jnp.broadcast_to(acc[0:1].astype(I32) - 1, (8, 128))
        list_lane[...] = jnp.broadcast_to(acc[1:2].astype(I32), (8, 128))
        name = acc[2:3] * 4096.0 + acc[3:4] * 128.0 + acc[4:5]
        name = jnp.broadcast_to(jnp.where(acc[0:1] > 0.5, name, -1.0), (128, 128))
        other = iota((128, 128), 0) != iota((128, 128), 1)
        same = jnp.logical_and(jnp.logical_and(name == name.T, name >= 0.0), other)
        mates[...] = jnp.where(same, 1.0, 0.0).astype(BF16)
        return jnp.where(most > 127.5, 1.0, 0.0)

    def joined(f):
        got = jnp.zeros((8, 128), F32)
        for g in range(4):
            v = lanes_of(f[8 * g : 8 * g + 8, :], list_lane[...])
            got = got + jnp.where(list_row[...] == iota((8, 128), 0) + 8 * g, v, 0.0)
        got = jnp.sum(got, axis=0, keepdims=True)
        p0 = got.astype(BF16).astype(F32)
        p1 = (got - p0).astype(BF16).astype(F32)
        p = jnp.concatenate([p0, p1, got - p0 - p1, jnp.zeros((13, 128), F32)], axis=0).astype(BF16)
        o = dot_nn(p, mates[...])
        more = jnp.broadcast_to((o[0:1] + o[1:2]) + o[2:3], (8, 128))
        outs = []
        for g in range(4):
            at = place_of[8 * g : 8 * g + 8, :]
            v = lanes_of(more, jnp.maximum(at, 0) & 127)
            outs.append(f[8 * g : 8 * g + 8, :] + jnp.where(at >= 0, v, 0.0))
        return jnp.concatenate(outs, axis=0)

    def dot_all(v):
        return jnp.sum(jnp.sum(v, axis=0, keepdims=True), axis=1, keepdims=True)

    def spread(v):
        return jnp.broadcast_to(v, (8, 128))

    zero = jnp.zeros((8, 128), F32)
    gather(kf, slots)
    gather(xf, slots2)
    k_own, t_own = to_entries(slots), to_entries(slots2)
    wo[...] = k_own
    zo[...] = t_own
    round0 = [k_own, t_own, ids]
    pl.semaphore_wait(barrier, 127)
    lrcv[pl.ds(me, 1)] = lsnd[pl.ds(me, 1)]
    for n, (px, py, p) in enumerate(others):
        if n == 48:
            send(0, round0)
        pltpu.make_async_remote_copy(
            src_ref=lsnd.at[pl.ds(p, 1)], dst_ref=lrcv.at[pl.ds(me, 1)],
            send_sem=lssem, recv_sem=lrsem, device_id=(px, py), device_id_type=MESH,
        ).start()
    many = same_cell()
    msgs[...] = receive(0)
    gface[...] = area[...] * 0.5 * (wo[...] + msgs[0:32, :])
    flows[...] = gface[...] * (zo[...] - msgs[32:64, :])
    to_slots(flows, slots)
    scatter(slots)
    tids = msgs[64:72, :].astype(I32)
    for j in range(8):
        oht[:, pl.ds(128 * j, 128)] = (iota((1024, 128), 0) == tids[j : j + 1]).astype(F32).astype(BF16)

    def first(k, c):
        at = pl.ds(8 * k, 8)

        def emit(c, a):
            rb[c, at, :] = a + nat[pl.ds(512 * k + c, 8, stride=64), :]

        stencil(k, lambda c: xf[c, at, :], emit, False)
        return c

    lax.fori_loop(0, 4, first, 0)
    laser().wait_recv()
    by_rank = []
    for j in range(8):
        by_rank.append(lrcv[:, j, :])
    pieces = thirds(jnp.concatenate(by_rank, axis=0))
    for q in range(8):
        o = oht[pl.ds(128 * q, 128), :]
        h = (dot_nn(o, pieces[0]) + dot_nn(o, pieces[1])) + dot_nn(o, pieces[2])
        for part in range(4):
            heat[pl.ds(512 * q + part, 128, stride=4), :] = h[:, 64 * part : 64 * part + 64]
        for b in range(4 * q, 4 * q + 4):
            en[64 * b : 64 * b + 64, :] = heat[128 * b : 128 * b + 128, :].T

    def start(k, c):
        at = pl.ds(8 * k, 8)
        for c in range(64):
            ra[c, at, :] = en[pl.ds(512 * k + c, 8, stride=64), :] - rb[c, at, :]
        return 0

    lax.fori_loop(0, 4, start, 0)
    gather(ra, slots2)
    ro[...] = to_entries(slots2)
    send(1, [ro[...], spread(jnp.maximum(over, many))])

    def early(k, sums):
        at = pl.ds(8 * k, 8)
        s = list(sums)

        def emit(c, a):
            r = ra[c, at, :]
            wf[c, at, :] = a
            s[0] = s[0] + r * r
            s[1] = s[1] + r * a

        stencil(k, lambda c: ra[c, at, :], emit, True)
        return tuple(s)

    rr, rw = [dot_all(v) for v in lax.fori_loop(0, 4, early, (zero, zero))]
    gather(wf, slots2)
    wo[...] = to_entries(slots2)
    msgs[...] = receive(1)
    flag_out[...] = jnp.max(msgs[32:33, :], axis=1, keepdims=True)
    flux = gface[...] * (ro[...] - msgs[0:32, :])
    flows[...] = flux
    rw = rw + dot_all(ro[...] * flux)
    wo[...] = wo[...] + joined(flux)

    old_rr = old_alpha = alpha1 = beta1 = None
    r_now, r_next = ra, rb
    for it in range(ITERS):
        last = it == ITERS - 1
        if last:
            send(it + 2, [spread(rr), spread(rw)])
        else:
            send(it + 2, [wo[...], spread(rr), spread(rw)])
        to_slots(flows, slots)
        scatter(slots)
        if it:
            r_now, r_next = r_next, r_now
            alpha, beta = spread(alpha1), None if it == 1 else spread(beta1)

        def along(k, sums, it=it, last=last, r_now=r_now, r_next=r_next):
            at = pl.ds(8 * k, 8)
            d = list(sums)

            def load(c):
                here = nat[pl.ds(512 * k + c, 8, stride=64), :]
                if it == 0:
                    w = wf[c, at, :] + here
                    wf[c, at, :] = w
                    d[2] = d[2] + w * w
                    return w
                w = wf[c, at, :]
                z = uf[c, at, :] + here
                s = w
                r = r_next[c, at, :]
                q = r
                if it > 1:
                    z = z + beta * zf[c, at, :]
                    s = s + beta * sf[c, at, :]
                    q = q + beta * pf[c, at, :]
                pf[c, at, :] = q
                xf[c, at, :] = xf[c, at, :] + alpha * q
                sf[c, at, :] = s
                r = r - alpha * s
                w = w - alpha * z
                r_now[c, at, :] = r
                wf[c, at, :] = w
                if not last:
                    zf[c, at, :] = z
                    for n, (p, q) in enumerate(((r, r), (r, w), (w, w), (r, s), (w, s), (s, s), (w, z), (s, z))):
                        d[n] = d[n] + p * q
                return w

            def emit(c, a):
                uf[c, at, :] = a
                d[8] = d[8] + wf[c, at, :] * a

            if last:
                for c in range(64):
                    load(c)
            else:
                stencil(k, load, emit, True)
            return tuple(d)

        dots = lax.fori_loop(0, 4, along, (zero,) * 9)
        if last:
            outs = [
                pltpu.make_async_copy(src, dst, out_sem.at[n])
                for n, (src, dst) in enumerate(zip((xf, r_now, pf, wf, sf), (x_out, r_out, p_out, w_out, s_out)))
            ]
            for c in outs:
                c.start()
        else:
            dots = [dot_all(v) for v in dots]
            if it == 0:
                dots[0], dots[1] = rr, rw
            gather(uf, slots2)
            ro[...] = to_entries(slots2)
        msgs[...] = receive(it + 2)
        base = 0 if last else 32
        g_rr, g_rw = total(msgs[base : base + 1, :]), total(msgs[base + 8 : base + 9, :])
        if it:
            beta1 = g_rr / old_rr
            alpha1 = g_rr / (g_rw - beta1 * g_rr / old_alpha)
        else:
            alpha1 = g_rr / g_rw
        old_rr, old_alpha = g_rr, alpha1
        if last:
            break
        flux = gface[...] * (wo[...] - msgs[0:32, :])
        flows[...] = flux
        rr, rw, ww, rs, ws, ss, wz, sz, wu = dots
        wq = wu + dot_all(wo[...] * flux)
        z = ro[...] + joined(flux)
        s = wo[...]
        if it:
            z = z + beta1 * zo[...]
            rs = rw + beta1 * rs
            ss = ww + beta1 * (2.0 * ws + beta1 * ss)
            sz = wq + beta1 * (2.0 * wz + beta1 * sz)
            ws = ww + beta1 * ws
        else:
            rs, ss, sz, ws = rw, ww, wq, ww
        zo[...] = z
        wo[...] = s - alpha1 * z
        rr = rr + alpha1 * (alpha1 * ss - 2.0 * rs)
        rw = rw + alpha1 * (alpha1 * sz - 2.0 * ws)

    scale_out[0:8, :] = spread(alpha1)
    scale_out[8:16, :] = spread(beta1)
    for r in range(ROUNDS):
        all_of(r).wait_send()
    laser().wait_send()
    for c in outs:
        c.wait()


def finish_kernel(scale, x, r, p, w, s, x_out, r_out):
    alpha, beta = scale[0:8, :], scale[8:16, :]
    for c in range(16):
        for k in range(4):
            at, to = pl.ds(8 * k, 8), pl.ds(64 * k + c % 8, 8, stride=8)
            x_out[c // 8, to, :] = x[c, at, :] + alpha * (r[c, at, :] + beta * p[c, at, :])
            r_out[c // 8, to, :] = r[c, at, :] - alpha * (w[c, at, :] + beta * s[c, at, :])


def finish(scale, *fields):
    of = pl.BlockSpec((16, 32, 128), lambda k: (k, 0, 0))
    to = pl.BlockSpec((2, 256, 128), lambda k: (k, 0, 0))
    x, r = pl.pallas_call(
        finish_kernel,
        grid=(4,),
        out_shape=[jax.ShapeDtypeStruct((8, 256, 128), F32)] * 2,
        in_specs=[pl.BlockSpec((16, 128), lambda k: (0, 0))] + [of] * 5,
        out_specs=[to] * 2,
    )(scale, *fields)
    return untiled(x), untiled(r)


def tiled(v):
    return v.reshape(8, 8, 32, 128).transpose(0, 2, 1, 3).reshape(2048, 128)


def untiled(v):
    return v.reshape(8, 32, 8, 128).transpose(0, 2, 1, 3).reshape(64, 4096)


def vm(*shape, dtype=F32):
    return pltpu.VMEM(shape, dtype)


def shards(*args):
    temp, base, store, level, face, area, rows, owner, tile = args
    field = lambda: vm(64, 32, 128)
    part = lambda: vm(48, 32, 128)
    slot = lambda dtype=F32: vm(64, 128, dtype=dtype)
    *fields, flag, scale = pl.pallas_call(
        step_kernel,
        out_shape=[
            *[jax.ShapeDtypeStruct((64, 32, 128), F32)] * 5,
            jax.ShapeDtypeStruct((1, 1), F32),
            jax.ShapeDtypeStruct((16, 128), F32),
        ],
        in_specs=[pl.BlockSpec(memory_space=pl.ANY)] * 9,
        out_specs=[pl.BlockSpec(memory_space=pl.ANY)] * 5 + [pl.BlockSpec(memory_space=pltpu.VMEM)] * 2,
        scratch_shapes=[
            vm(2048, 128), vm(2048, 128), vm(2048, 128),
            vm(32, 128, dtype=I32), vm(32, 128, dtype=I32), vm(32, 128), vm(256, 256),
            vm(1, 256, dtype=I32), vm(1, 256, dtype=I32),
            field(), field(), field(), part(), part(), part(),
            field(), field(), field(), field(), field(), vm(2048, 128), vm(2048, 128),
            vm(1024, 128, dtype=BF16), vm(32, 128, 256, dtype=BF16),
            slot(I32), slot(I32), slot(I32), slot(I32), vm(32, 128, dtype=I32), vm(32, 128, dtype=I32),
            slot(), slot(), vm(128, 128),
            vm(32, 128), vm(32, 128), vm(32, 128), vm(32, 128), vm(32, 128), vm(4096, 64), vm(1024, 1024, dtype=BF16),
            field(), field(), vm(128, 64), slot(), vm(32, 128, dtype=I32), vm(8, 128, dtype=I32), vm(8, 128, dtype=I32), vm(128, 128, dtype=BF16),
            vm(ROUNDS, 128, 128), vm(ROUNDS, 128, 128), vm(128, 8, 256), vm(128, 8, 256),
            pltpu.SemaphoreType.DMA((9,)),
            pltpu.SemaphoreType.DMA((ROUNDS,)),
            pltpu.SemaphoreType.DMA((ROUNDS,)),
            pltpu.SemaphoreType.DMA,
            pltpu.SemaphoreType.DMA,
            pltpu.SemaphoreType.DMA((5,)),
        ],
        compiler_params=pltpu.CompilerParams(
            collective_id=0, has_side_effects=True, vmem_limit_bytes=63 * 1024 * 1024
        ),
    )(
        tiled(temp), tiled(base), tiled(store), level.reshape(32, 128),
        face[0].T, area[0].T, rows[0], owner.reshape(1, 256), tile,
    )
    return lax.cond(
        flag[0, 0] > 0.5,
        lambda: general(*args),
        lambda: finish(scale, *fields),
    )


def solution(mesh):
    return jax.shard_map(
        shards,
        mesh=mesh,
        in_specs=(
            P(None, ("bx", "by")),
            P(None, ("bx", "by")),
            P(None, ("bx", "by")),
            P(("bx", "by")),
            P(("bx", "by"), None, None),
            P(("bx", "by"), None, None),
            P(None, ("bx", "by"), None),
            P(None, ("bx", "by"), None),
            P(None, ("bx", "by")),
        ),
        out_specs=(P(None, ("bx", "by")), P(None, ("bx", "by"))),
        check_vma=False,
    )
```
